32 devices in a mesh: grp: 4 (over y, core), tile: 8 (over z, x).
Axes of the slice: x: 2, y: 2, z: 4, core: 2. Of those that a mesh axis runs over, the one named last changes fastest.
Arguments:
- amplitudes: bfloat16 [256, 4, 9216], P(('grp', 'tile')), may hold values from -6 to 6
- kept: int32 [256, 4], P(('grp', 'tile')), may hold values from 0 to 7, all different within a row; in each aligned block of 8 rows (0 to 7, 8 to 15, ...) at most 8 rows name the same one
- coef: bfloat16 [256], P(('grp', 'tile')), may hold values from -0.125 to 0.125
- ladder_factor: bfloat16 [8, 16, 96, 96], P('tile'), may hold values from -0.375 to 0.375
- cycle_integral_tiles: bfloat16 [8, 96, 96], P('tile'), may hold values from -0.625 to 0.625
Outputs:
- residual: bfloat16 [256, 4, 9216], P(('grp', 'tile'))
The draws below stay inside these ranges and needn't reach their ends.
Inputs may be any that keep to these rules, and one draw needn't show every extreme that they name: `kept`: each row names 4 different tiles; in each aligned block of 8 rows (the pairs of one device) no tile is named by more than 8 rows, a bound that some block reaches.
All inputs are finite; a program needn't handle non-finite values.
Results may differ from the reference program's by a relative error of at most 0.0056.
Values may be sent and summed in bfloat16 or wider, within the bound.
No kernel may reach another device: no remote copies, remote signals or barrier semaphores. Data moves between devices by JAX's collectives and lax.ppermute only.
A program may use at most 128 MiB of HBM per device.

```python
import math
import jax
import jax.numpy as jnp
import numpy as np
from jax import lax

TS = 96
NF = 16
K = 4
PD = 8
NVT = 8
PAIRS = 256
CAP = 8


def shard_levels(rng, shape, cuts, low, high):
    def one(axis_at, parts):
        steps = jax.random.uniform(jax.random.fold_in(jax.random.fold_in(rng, 6), axis_at), (parts,), jnp.float32, low / len(cuts), high / len(cuts))
        return jnp.repeat(jnp.exp(steps), shape[axis_at] // parts).reshape((-1,) + (1,) * (len(shape) - axis_at - 1))

    loudness = one(*cuts[0])
    for cut in cuts[1:]:
        loudness = loudness * one(*cut)
    return loudness


def routed_block(key, own, number, rows, count, top, most, lean):
    sequence = jax.random.permutation(key, count)
    packed, usual = shares(count, rows * top, most, lean, True), shares(count, rows * top, most, lean, False)
    places = jnp.arange(count)

    def named(lengths, turn):
        used = int((lengths > 0).sum())
        fixed = max(1, used // 4)
        passed = fixed + (places - fixed + turn * (used - fixed)) % max(1, count - fixed)
        return jnp.zeros((count,), jnp.int32).at[sequence[jnp.where(places < fixed, places, passed)]].set(jnp.asarray(lengths, jnp.int32))

    lengths = jnp.where(number % 4 == 0, named(packed, number // 4), named(usual, number - number // 4 - 1))
    mixed = jax.random.permutation(jax.random.fold_in(own, 3), count)
    source_of, sink = mixed[0:count // 2 * 2:2], mixed[1:count // 2 * 2:2]
    margin = jnp.minimum(lengths[source_of] - 1, most - lengths[sink]) // 2
    margin = jnp.where((source_of == sequence[0]) | (sink == sequence[0]) | (lengths[sink] == 0), 0, jnp.maximum(margin, 0))
    passed = jax.random.randint(jax.random.fold_in(own, 4), (count // 2,), 0, 1 << 20) % (margin + 1)
    lengths = lengths.at[source_of].add(-passed).at[sink].add(passed)
    items = jnp.searchsorted(jnp.cumsum(lengths), jnp.arange(rows * top), side="right").astype(jnp.int32)
    grid = items.reshape(top, rows).T
    grid = grid[jax.random.permutation(jax.random.fold_in(own, 1), rows)]
    turn = jax.random.randint(jax.random.fold_in(own, 2), (rows, 1), 0, top)
    return jnp.take_along_axis(grid, (jnp.arange(top)[None, :] + turn) % top, axis=1)


def shares(amount, total, bound, skew, full):
    portions = [(1 << 20) // math.isqrt(standing ** skew) + 1 for standing in range(1, amount + 1)]
    largest = bound if full else min(bound, max(-(-total // amount), total * portions[0] // sum(portions)))
    least = 1 if total - largest >= amount - 1 else 0
    given, surplus = [largest] + [least] * (amount - 1), total - largest - least * (amount - 1)
    while surplus > 0:
        candidates = [i for i in range(1, amount) if given[i] < largest] or [i for i in range(1, amount) if given[i] < bound]
        whole, left = sum([portions[i] for i in candidates]), surplus
        for i in candidates:
            extra = min(bound - given[i], max(1, left * portions[i] // whole), surplus)
            given[i] = given[i] + extra
            surplus = surplus - extra
    return np.array(given)


def scatter_about(own_key, shape, width, bound, shards=(), held_as=jnp.bfloat16):
    array = jax.random.normal(own_key, shape, jnp.float32) * width
    if len(shards) > 0:
        array = shard_levels(own_key, shape, shards, -0.22, 0.18) * array
    return jnp.clip(array, min=-bound, max=bound).astype(held_as)


def setup_inputs(seed: int = 0) -> dict:
    key_list = jax.random.split(jax.random.key(seed), 6)
    amplitudes = scatter_about(key_list[0], (PAIRS, K, TS * TS), 1.0, 6.0, ((0, 32),))
    kept_keys = jax.random.split(jax.random.fold_in(key_list[1], 1), PAIRS // PD)
    kept_turns = jax.random.permutation(jax.random.fold_in(key_list[1], 3), PAIRS // PD)
    kept = jax.vmap(lambda own, number: routed_block(jax.random.fold_in(key_list[1], 2), own, number, PD, NVT, K, CAP, 2))(kept_keys, kept_turns).reshape((PAIRS, K))
    coef = scatter_about(key_list[2], (PAIRS,), ((PAIRS * K * TS // NVT) ** -0.5), 0.125, ((0, 32),))
    ladder_factor = scatter_about(key_list[3], (NVT, NF, TS, TS), (TS * 3) ** -0.5, 0.375, ((0, 8),))
    cycle_integral_tiles = scatter_about(key_list[4], (NVT, TS, TS), TS ** -0.5, 0.625, ((0, 8),))
    return {"amplitudes": amplitudes, "kept": kept, "coef": coef, "ladder_factor": ladder_factor, "cycle_integral_tiles": cycle_integral_tiles}


def block_terms(block_list, factors, hidden_state):
    highest_precision = lax.Precision.HIGHEST
    blocks_wide = block_list.astype(jnp.float32)
    total = jnp.einsum("pkab,pkbc->pkac", blocks_wide, hidden_state.astype(jnp.float32), precision=highest_precision)
    for number in range(NF):
        factor = factors[:, :, number].astype(jnp.float32)
        inner = jnp.einsum("pkab,pkcb->pkac", blocks_wide, factor, precision=highest_precision).astype(jnp.bfloat16)
        inner = lax.optimization_barrier(inner).astype(jnp.float32)
        total = total + jnp.einsum("pkda,pkac->pkdc", factor, inner, precision=highest_precision)
    return total.astype(jnp.bfloat16)


def reference(amplitudes, kept, coef, ladder_factor, cycle_integral_tiles):
    highest_precision = lax.Precision.HIGHEST
    groups = PAIRS // PD
    tiles = jnp.arange(NVT, dtype=jnp.int32)
    amps = amplitudes.reshape(groups, PD, K, TS, TS)
    ids = kept.reshape(groups, PD, K).astype(jnp.int32)
    weights = coef.reshape(groups, PD)

    def accumulate(loop_carry, args):
        block_list, rows, scales = args
        one_hot_selector = (rows[:, :, None] == tiles[None, None, :]).astype(jnp.float32) * scales.astype(jnp.float32)[:, None, None]
        return loop_carry + jnp.einsum("nti,ntgh->igh", one_hot_selector, block_list.astype(jnp.float32), precision=highest_precision), None

    start = jnp.zeros((NVT, TS, TS), jnp.float32)
    cycle_total, _ = lax.scan(accumulate, start, (amps, ids, weights))
    cycle_running_sum = cycle_total.astype(jnp.bfloat16)
    hidden_state = jnp.einsum("rwq,rqj->rwj", cycle_running_sum.astype(jnp.float32), cycle_integral_tiles.astype(jnp.float32), precision=highest_precision).astype(jnp.bfloat16)

    def one_group(args):
        block_list, rows = args
        return block_terms(block_list, ladder_factor[rows], hidden_state[rows])

    result = lax.map(one_group, (amps, ids))
    return result.reshape(PAIRS, K, TS * TS)
```

```python
import functools

import jax
import jax.numpy as jnp
from jax import lax
from jax.experimental import pallas as pl
from jax.experimental.pallas import tpu as pltpu
from jax.sharding import PartitionSpec as P

LANES = 128
ALL = ("grp", "tile")


def pack_factors(factors):
    count, width, _ = factors.shape
    quads = factors.reshape(count // 4, 4, width, width)
    spare = LANES - width
    pieces = [quads[:, 3, :, i * spare:(i + 1) * spare] for i in range(3)]
    packed = jnp.concatenate([quads[:, :3], jnp.stack(pieces, axis=1)], axis=-1)
    return packed.reshape(2, count // 8 * 3, width, LANES)


def unpack(refs, stacked, beside, width):
    spare = LANES - width
    lane = lax.broadcasted_iota(jnp.int32, (width, LANES), 1)
    number = 0
    for ref in refs:
        for quad in range(ref.shape[0] // 3):
            parts = [ref[quad * 3 + i] for i in range(3)]
            wide = [part.astype(jnp.float32) for part in parts]
            moved = [pltpu.roll(wide[i], spare * (i + 1), 1) for i in range(3)]
            fourth = jnp.where(lane < spare, moved[0], jnp.where(lane < 2 * spare, moved[1], moved[2]))
            parts.append(fourth.astype(jnp.bfloat16))
            for part in parts:
                stacked[number * width:(number + 1) * width, :] = part
                beside[:, number * LANES:(number + 1) * LANES] = part
                number += 1


def ladder_kernel(tiles, width, kept_ref, me_ref, blocks_ref, hidden_ref, *rest):
    factor_refs, out_ref = rest[:2 * tiles], rest[2 * tiles]
    table, counts, stacked, beside, grown = rest[2 * tiles + 1:]
    rows = blocks_ref.shape[0]
    most = table.shape[0] // tiles
    me = me_ref[0]

    def clear(j, _):
        counts[j] = 0
        return 0

    lax.fori_loop(0, tiles, clear, 0)

    def fill(r, _):
        slot = kept_ref[r] ^ me
        n = counts[slot]
        table[slot * most + n] = r
        counts[slot] = n + 1
        return 0

    lax.fori_loop(0, rows, fill, 0)

    factor_count = stacked.shape[0] // width
    for slot in range(tiles):
        count = counts[slot]

        @pl.when(count > 0)
        def _(slot=slot, count=count):
            unpack(factor_refs[2 * slot:2 * slot + 2], stacked, beside, width)
            hidden = hidden_ref[slot ^ me]

            def job(i, _):
                first = table[slot * most + 2 * i]
                second = table[slot * most + jnp.minimum(2 * i + 1, count - 1)]
                left, right = blocks_ref[first], blocks_ref[second]
                pair = jnp.concatenate([left, right], axis=1)
                inner = jnp.dot(stacked[...], pair, preferred_element_type=jnp.float32)
                for f in range(factor_count):
                    part = inner[f * width:(f + 1) * width].astype(jnp.bfloat16)
                    grown[0:width, f * LANES:(f + 1) * LANES] = part[:, :LANES]
                    grown[width:2 * width, f * LANES:(f + 1) * LANES] = part[:, LANES:]
                total = lax.dot_general(
                    grown[...], beside[...], (((1,), (1,)), ((), ())), preferred_element_type=jnp.float32
                )
                both = jnp.concatenate([left[:width], right[:width]], axis=0)
                total = total + jnp.dot(both, hidden, preferred_element_type=jnp.float32)
                total = total.astype(jnp.bfloat16)
                out_ref[first] = total[:width]
                out_ref[second] = total[width:]
                return 0

            lax.fori_loop(0, (count + 1) // 2, job, 0)


def ladder(kept, me, blocks, hidden, parts, tiles, width, most):
    rows = blocks.shape[0]
    factor_count = parts[0].shape[0] // 3 * 4 * 2
    smem, vmem = pl.BlockSpec(memory_space=pltpu.SMEM), pl.BlockSpec(memory_space=pltpu.VMEM)
    return pl.pallas_call(
        functools.partial(ladder_kernel, tiles, width),
        out_shape=jax.ShapeDtypeStruct((rows, width, width), jnp.bfloat16),
        in_specs=[smem, smem] + [vmem] * (2 + len(parts)),
        out_specs=vmem,
        scratch_shapes=[
            pltpu.SMEM((tiles * most,), jnp.int32),
            pltpu.SMEM((tiles,), jnp.int32),
            pltpu.VMEM((factor_count * width, LANES), jnp.bfloat16),
            pltpu.VMEM((width, factor_count * LANES), jnp.bfloat16),
            pltpu.VMEM((2 * width, factor_count * LANES), jnp.bfloat16),
        ],
        compiler_params=pltpu.CompilerParams(vmem_limit_bytes=48 << 20),
        cost_estimate=pl.CostEstimate(flops=rows * factor_count * 4 * width**3, bytes_accessed=4 << 20, transcendentals=0),
    )(kept, me, blocks, hidden, *parts)


def on_device(amplitudes, kept, coef, ladder_factor, cycle_integral_tiles):
    pairs, slots, flat = amplitudes.shape
    width = ladder_factor.shape[-1]
    tiles, groups = lax.axis_size("tile"), lax.axis_size("grp")
    across = 1 << ((tiles.bit_length() - 1) // 2)
    rows = pairs * slots
    me = lax.axis_index("tile")
    core = lax.axis_index("grp") % 2

    def to_tile(array, flip):
        return lax.ppermute(array, "tile", [(i, i ^ flip) for i in range(tiles)])

    def to_core(array):
        return lax.ppermute(array, "grp", [(i, i ^ 1) for i in range(groups)])

    packed = pack_factors(ladder_factor[0])
    mine = lax.dynamic_index_in_dim(packed, core, 0, keepdims=False)
    halves = {0: mine}
    for up in range(1, tiles // across):
        halves[up * across] = to_tile(mine, up * across)
    for up in range(tiles // across):
        for side in range(1, across):
            halves[up * across + side] = to_tile(halves[up * across], side)
    parts = []
    for slot in range(tiles):
        if slot == 0:
            parts += [packed[0], packed[1]]
        else:
            parts += [halves[slot], to_core(halves[slot])]

    block_list = amplitudes.reshape(rows, flat)
    names = kept.reshape(rows)
    weights = jnp.where(
        jnp.arange(tiles, dtype=jnp.int32)[:, None] == names[None, :], jnp.repeat(coef, slots)[None, :], jnp.zeros((), coef.dtype)
    )
    part_sum = jnp.dot(weights, block_list, preferred_element_type=jnp.float32)
    share = flat // groups
    shares = part_sum.reshape(tiles, groups, share).transpose(1, 0, 2).reshape(groups * tiles, share)
    arrived = lax.all_to_all(shares, ALL, split_axis=0, concat_axis=0, tiled=True)
    running = jnp.sum(arrived, axis=0).astype(jnp.bfloat16).reshape(width // groups, width)
    hidden = jnp.dot(running, cycle_integral_tiles[0], preferred_element_type=jnp.float32).astype(jnp.bfloat16)
    hidden = jnp.pad(hidden, ((0, 0), (0, LANES - width)))
    spread = lax.all_to_all(
        jnp.broadcast_to(hidden[None], (groups * tiles,) + hidden.shape), ALL, split_axis=0, concat_axis=0, tiled=True
    )
    hidden = spread.reshape(groups, tiles, width // groups, LANES).transpose(1, 0, 2, 3).reshape(tiles, width, LANES)
    hidden = jnp.pad(hidden, ((0, 0), (0, LANES - width), (0, 0)))[:, :, :width]

    blocks = jnp.pad(block_list.reshape(rows, width, width), ((0, 0), (0, LANES - width), (0, LANES - width)))
    residual = ladder(names, me.reshape(1), blocks, hidden, parts, tiles, width, pairs)
    return residual.reshape(pairs, slots, flat)


def solution(mesh):
    in_specs = (
        P(("grp", "tile"), None, None),
        P(("grp", "tile"), None),
        P(("grp", "tile")),
        P("tile", None, None, None),
        P("tile", None, None),
    )
    out_specs = P(("grp", "tile"), None, None)
    return jax.shard_map(
        on_device, mesh=mesh, in_specs=in_specs, out_specs=out_specs, check_vma=False
    )
```

```python
import functools

import jax
import jax.numpy as jnp
from jax import lax
from jax.experimental import pallas as pl
from jax.experimental.pallas import tpu as pltpu
from jax.sharding import PartitionSpec as P

LANES = 128
ALL = ("grp", "tile")


def pack_factors(factors):
    count, width, _ = factors.shape
    quads = factors.reshape(count // 4, 4, width, width)
    spare = LANES - width
    pieces = [quads[:, 3, :, i * spare:(i + 1) * spare] for i in range(3)]
    packed = jnp.concatenate([quads[:, :3], jnp.stack(pieces, axis=1)], axis=-1)
    return packed.reshape(2, count // 8 * 3, width, LANES)


def unpack(refs, stacked, beside, width):
    spare = LANES - width
    lane = lax.broadcasted_iota(jnp.int32, (width, LANES), 1)
    number = 0
    for ref in refs:
        for quad in range(ref.shape[0] // 3):
            parts = [ref[quad * 3 + i] for i in range(3)]
            wide = [part.astype(jnp.float32) for part in parts]
            moved = [pltpu.roll(wide[i], spare * (i + 1), 1) for i in range(3)]
            fourth = jnp.where(lane < spare, moved[0], jnp.where(lane < 2 * spare, moved[1], moved[2]))
            parts.append(fourth.astype(jnp.bfloat16))
            for part in parts:
                stacked[number * width:(number + 1) * width, :] = part
                beside[:, number * LANES:(number + 1) * LANES] = part
                number += 1


def ladder_kernel(near, tiles, width, first_stage, kept_ref, me_ref, blocks_ref, *rest):
    if not first_stage:
        rest = rest[1:]
    factor_refs, total_ref = rest[:2 * len(near)], rest[2 * len(near)]
    table, counts, stacked, beside, grown = rest[2 * len(near) + 1:]
    rows = blocks_ref.shape[0]
    most = table.shape[0] // tiles
    me = me_ref[0]

    def clear(j, _):
        counts[j] = 0
        return 0

    lax.fori_loop(0, tiles, clear, 0)

    def fill(r, _):
        slot = kept_ref[r] ^ me
        n = counts[slot]
        table[slot * most + n] = r
        counts[slot] = n + 1
        return 0

    lax.fori_loop(0, rows, fill, 0)

    factor_count = stacked.shape[0] // width
    for number, slot in enumerate(near):
        count = counts[slot]

        @pl.when(count > 0)
        def _(number=number, slot=slot, count=count):
            unpack(factor_refs[2 * number:2 * number + 2], stacked, beside, width)

            def job(i, _):
                first = table[slot * most + 2 * i]
                second = table[slot * most + jnp.minimum(2 * i + 1, count - 1)]
                pair = jnp.concatenate([blocks_ref[first], blocks_ref[second]], axis=1)
                inner = jnp.dot(stacked[...], pair, preferred_element_type=jnp.float32)
                for f in range(factor_count):
                    part = inner[f * width:(f + 1) * width].astype(jnp.bfloat16)
                    grown[0:width, f * LANES:(f + 1) * LANES] = part[:, :LANES]
                    grown[width:2 * width, f * LANES:(f + 1) * LANES] = part[:, LANES:]
                total = lax.dot_general(
                    grown[...], beside[...], (((1,), (1,)), ((), ())), preferred_element_type=jnp.float32
                )
                total_ref[first] = total[:width]
                total_ref[second] = total[width:]
                return 0

            lax.fori_loop(0, (count + 1) // 2, job, 0)


SMEM, VMEM = pl.BlockSpec(memory_space=pltpu.SMEM), pl.BlockSpec(memory_space=pltpu.VMEM)


def ladder(near, kept, me, blocks, total, parts, tiles, width, most):
    rows = blocks.shape[0]
    factor_count = parts[0].shape[0] // 3 * 4 * 2
    carried = [] if total is None else [total]
    return pl.pallas_call(
        functools.partial(ladder_kernel, near, tiles, width, total is None),
        out_shape=jax.ShapeDtypeStruct((rows, width, width), jnp.float32),
        in_specs=[SMEM, SMEM] + [VMEM] * (1 + len(carried) + len(parts)),
        out_specs=VMEM,
        input_output_aliases={} if total is None else {3: 0},
        scratch_shapes=[
            pltpu.SMEM((tiles * most,), jnp.int32),
            pltpu.SMEM((tiles,), jnp.int32),
            pltpu.VMEM((factor_count * width, LANES), jnp.bfloat16),
            pltpu.VMEM((width, factor_count * LANES), jnp.bfloat16),
            pltpu.VMEM((2 * width, factor_count * LANES), jnp.bfloat16),
        ],
        compiler_params=pltpu.CompilerParams(vmem_limit_bytes=12 << 20),
        cost_estimate=pl.CostEstimate(
            flops=16 * rows * factor_count * 4 * width**3 * len(near) // tiles, bytes_accessed=1 << 20, transcendentals=0
        ),
    )(kept, me, blocks, *carried, *parts)


def close_kernel(tiles, width, kept_ref, blocks_ref, total_ref, spread_ref, out_ref, hidden):
    groups = spread_ref.shape[0] // tiles
    hidden[:, width:, :] = jnp.zeros((tiles, LANES - width, LANES), jnp.bfloat16)
    for tile in range(tiles):
        pieces = [spread_ref[g * tiles + tile].astype(jnp.float32) for g in range(groups)]
        hidden[tile, :width, :] = jnp.concatenate(pieces, axis=0).astype(jnp.bfloat16)
    for r in range(blocks_ref.shape[0]):
        term = jnp.dot(blocks_ref[r, :width, :], hidden[kept_ref[r]], preferred_element_type=jnp.float32)
        out_ref[r] = (total_ref[r] + term[:, :width]).astype(jnp.bfloat16)


def close(kept, blocks, total, spread, tiles, width):
    rows = blocks.shape[0]
    return pl.pallas_call(
        functools.partial(close_kernel, tiles, width),
        out_shape=jax.ShapeDtypeStruct((rows, width, width), jnp.bfloat16),
        in_specs=[SMEM] + [VMEM] * 3,
        out_specs=VMEM,
        scratch_shapes=[pltpu.VMEM((tiles, LANES, LANES), jnp.bfloat16)],
        compiler_params=pltpu.CompilerParams(vmem_limit_bytes=16 << 20),
        cost_estimate=pl.CostEstimate(flops=rows * 2 * width**3, bytes_accessed=1 << 20, transcendentals=0),
    )(kept, blocks, total, spread)


def on_device(amplitudes, kept, coef, ladder_factor, cycle_integral_tiles):
    pairs, slots, flat = amplitudes.shape
    width = ladder_factor.shape[-1]
    tiles, groups = lax.axis_size("tile"), lax.axis_size("grp")
    across = 1 << ((tiles.bit_length() - 1) // 2)
    rows = pairs * slots
    me = lax.axis_index("tile")
    core = lax.axis_index("grp") % 2

    def to_tile(array, flip):
        return lax.ppermute(array, "tile", [(i, i ^ flip) for i in range(tiles)])

    def to_core(array):
        return lax.ppermute(array, "grp", [(i, i ^ 1) for i in range(groups)])

    block_list = amplitudes.reshape(rows, flat)
    names = kept.reshape(rows)
    weights = jnp.where(
        jnp.arange(tiles, dtype=jnp.int32)[:, None] == names[None, :], jnp.repeat(coef, slots)[None, :], jnp.zeros((), coef.dtype)
    )
    part_sum = jnp.dot(weights, block_list, preferred_element_type=jnp.float32)
    share = flat // groups
    shares = part_sum.reshape(tiles, groups, share).transpose(1, 0, 2).reshape(groups * tiles, share)
    arrived = lax.all_to_all(shares, ALL, split_axis=0, concat_axis=0, tiled=True)
    running = jnp.sum(arrived, axis=0).astype(jnp.bfloat16).reshape(width // groups, width)
    hidden = jnp.dot(running, cycle_integral_tiles[0], preferred_element_type=jnp.float32).astype(jnp.bfloat16)
    hidden = jnp.pad(hidden, ((0, 0), (0, LANES - width)))
    spread = lax.all_to_all(
        jnp.broadcast_to(hidden[None], (groups * tiles,) + hidden.shape), ALL, split_axis=0, concat_axis=0, tiled=True
    )

    packed = pack_factors(ladder_factor[0])
    mine = lax.dynamic_index_in_dim(packed, core, 0, keepdims=False)
    halves = {0: mine}
    for up in range(1, tiles // across):
        halves[up * across] = to_tile(mine, up * across)
    for up in range(tiles // across):
        source = halves[up * across]
        if up * across >= tiles // 2:
            source, _ = lax.optimization_barrier((source, hidden))
            halves[up * across] = source
        for side in range(1, across):
            halves[up * across + side] = to_tile(source, side)

    blocks = jnp.pad(block_list.reshape(rows, width, width), ((0, 0), (0, LANES - width), (0, LANES - width)))
    place = me.reshape(1)
    total = ladder((0,), names, place, blocks, None, [packed[0], packed[1]], tiles, width, pairs)
    for near in (tuple(range(1, tiles // 2)), tuple(range(tiles // 2, tiles))):
        parts = []
        for slot in near:
            parts += [halves[slot], to_core(halves[slot])]
        total, *parts = lax.optimization_barrier((total, *parts))
        total = ladder(near, names, place, blocks, total, parts, tiles, width, pairs)
    residual = close(names, blocks, total, spread, tiles, width)
    return residual.reshape(pairs, slots, flat)


def solution(mesh):
    in_specs = (
        P(("grp", "tile"), None, None),
        P(("grp", "tile"), None),
        P(("grp", "tile")),
        P("tile", None, None, None),
        P("tile", None, None),
    )
    out_specs = P(("grp", "tile"), None, None)
    return jax.shard_map(
        on_device, mesh=mesh, in_specs=in_specs, out_specs=out_specs, check_vma=False
    )
```

```python
import functools

import jax
import jax.numpy as jnp
from jax import lax
from jax.experimental import pallas as pl
from jax.experimental.pallas import tpu as pltpu
from jax.sharding import PartitionSpec as P

LANES = 128
ALL = ("grp", "tile")


def pack_factors(factors):
    count, width, _ = factors.shape
    quads = factors.reshape(count // 4, 4, width, width)
    spare = LANES - width
    pieces = [quads[:, 3, :, i * spare:(i + 1) * spare] for i in range(3)]
    packed = jnp.concatenate([quads[:, :3], jnp.stack(pieces, axis=1)], axis=-1)
    return packed.reshape(2, count // 8 * 3, width, LANES)


def unpack(refs, stacked, beside, width):
    spare = LANES - width
    lane = lax.broadcasted_iota(jnp.int32, (width, LANES), 1)
    number = 0
    for ref in refs:
        for quad in range(ref.shape[0] // 3):
            parts = [ref[quad * 3 + i] for i in range(3)]
            wide = [part.astype(jnp.float32) for part in parts]
            moved = [pltpu.roll(wide[i], spare * (i + 1), 1) for i in range(3)]
            fourth = jnp.where(lane < spare, moved[0], jnp.where(lane < 2 * spare, moved[1], moved[2]))
            parts.append(fourth.astype(jnp.bfloat16))
            for part in parts:
                stacked[number * width:(number + 1) * width, :] = part
                beside[:, number * LANES:(number + 1) * LANES] = part
                number += 1


def ladder_kernel(near, tiles, width, first_stage, kept_ref, me_ref, blocks_ref, *rest):
    if not first_stage:
        rest = rest[1:]
    factor_refs, total_ref = rest[:2 * len(near)], rest[2 * len(near)]
    table, counts, stacked, beside, grown = rest[2 * len(near) + 1:]
    rows = blocks_ref.shape[0]
    most = table.shape[0] // tiles
    me = me_ref[0]

    def clear(j, _):
        counts[j] = 0
        return 0

    lax.fori_loop(0, tiles, clear, 0)

    def fill(r, _):
        slot = kept_ref[r] ^ me
        n = counts[slot]
        table[slot * most + n] = r
        counts[slot] = n + 1
        return 0

    lax.fori_loop(0, rows, fill, 0)

    factor_count = stacked.shape[0] // width
    for number, slot in enumerate(near):
        count = counts[slot]

        @pl.when(count > 0)
        def _(number=number, slot=slot, count=count):
            unpack(factor_refs[2 * number:2 * number + 2], stacked, beside, width)

            def job(i, _):
                first = table[slot * most + 2 * i]
                second = table[slot * most + jnp.minimum(2 * i + 1, count - 1)]
                pair = jnp.concatenate([blocks_ref[first], blocks_ref[second]], axis=1)
                inner = jnp.dot(stacked[...], pair, preferred_element_type=jnp.float32)
                for f in range(factor_count):
                    part = inner[f * width:(f + 1) * width].astype(jnp.bfloat16)
                    grown[0:width, f * LANES:(f + 1) * LANES] = part[:, :LANES]
                    grown[width:2 * width, f * LANES:(f + 1) * LANES] = part[:, LANES:]
                total = lax.dot_general(
                    grown[...], beside[...], (((1,), (1,)), ((), ())), preferred_element_type=jnp.float32
                )
                total_ref[first] = total[:width]
                total_ref[second] = total[width:]
                return 0

            lax.fori_loop(0, (count + 1) // 2, job, 0)


SMEM, VMEM = pl.BlockSpec(memory_space=pltpu.SMEM), pl.BlockSpec(memory_space=pltpu.VMEM)


def ladder(near, kept, me, blocks, total, parts, tiles, width, most):
    rows = blocks.shape[0]
    factor_count = parts[0].shape[0] // 3 * 4 * 2
    carried = [] if total is None else [total]
    return pl.pallas_call(
        functools.partial(ladder_kernel, near, tiles, width, total is None),
        out_shape=jax.ShapeDtypeStruct((rows, width, width), jnp.float32),
        in_specs=[SMEM, SMEM] + [VMEM] * (1 + len(carried) + len(parts)),
        out_specs=VMEM,
        input_output_aliases={} if total is None else {3: 0},
        scratch_shapes=[
            pltpu.SMEM((tiles * most,), jnp.int32),
            pltpu.SMEM((tiles,), jnp.int32),
            pltpu.VMEM((factor_count * width, LANES), jnp.bfloat16),
            pltpu.VMEM((width, factor_count * LANES), jnp.bfloat16),
            pltpu.VMEM((2 * width, factor_count * LANES), jnp.bfloat16),
        ],
        compiler_params=pltpu.CompilerParams(vmem_limit_bytes=12 << 20),
        cost_estimate=pl.CostEstimate(
            flops=rows, bytes_accessed=rows, transcendentals=0
        ),
    )(kept, me, blocks, *carried, *parts)


def close_kernel(tiles, width, kept_ref, blocks_ref, total_ref, spread_ref, out_ref, hidden):
    groups = spread_ref.shape[0] // tiles
    hidden[:, width:, :] = jnp.zeros((tiles, LANES - width, LANES), jnp.bfloat16)
    for tile in range(tiles):
        pieces = [spread_ref[g * tiles + tile].astype(jnp.float32) for g in range(groups)]
        hidden[tile, :width, :] = jnp.concatenate(pieces, axis=0).astype(jnp.bfloat16)
    for r in range(blocks_ref.shape[0]):
        term = jnp.dot(blocks_ref[r, :width, :], hidden[kept_ref[r]], preferred_element_type=jnp.float32)
        out_ref[r] = (total_ref[r] + term[:, :width]).astype(jnp.bfloat16)


def close(kept, blocks, total, spread, tiles, width):
    rows = blocks.shape[0]
    return pl.pallas_call(
        functools.partial(close_kernel, tiles, width),
        out_shape=jax.ShapeDtypeStruct((rows, width, width), jnp.bfloat16),
        in_specs=[SMEM] + [VMEM] * 3,
        out_specs=VMEM,
        scratch_shapes=[pltpu.VMEM((tiles, LANES, LANES), jnp.bfloat16)],
        compiler_params=pltpu.CompilerParams(vmem_limit_bytes=16 << 20),
        cost_estimate=pl.CostEstimate(flops=rows * 2 * width**3, bytes_accessed=1 << 20, transcendentals=0),
    )(kept, blocks, total, spread)


def on_device(amplitudes, kept, coef, ladder_factor, cycle_integral_tiles):
    pairs, slots, flat = amplitudes.shape
    width = ladder_factor.shape[-1]
    tiles, groups = lax.axis_size("tile"), lax.axis_size("grp")
    across = 1 << ((tiles.bit_length() - 1) // 2)
    rows = pairs * slots
    me = lax.axis_index("tile")
    core = lax.axis_index("grp") % 2

    def to_tile(array, flip):
        return lax.ppermute(array, "tile", [(i, i ^ flip) for i in range(tiles)])

    def to_core(array):
        return lax.ppermute(array, "grp", [(i, i ^ 1) for i in range(groups)])

    block_list = amplitudes.reshape(rows, flat)
    names = kept.reshape(rows)
    weights = jnp.where(
        jnp.arange(tiles, dtype=jnp.int32)[:, None] == names[None, :], jnp.repeat(coef, slots)[None, :], jnp.zeros((), coef.dtype)
    )
    part_sum = jnp.dot(weights, block_list, preferred_element_type=jnp.float32)
    share = flat // groups
    shares = part_sum.reshape(tiles, groups, share).transpose(1, 0, 2).reshape(groups * tiles, share)
    arrived = lax.all_to_all(shares, ALL, split_axis=0, concat_axis=0, tiled=True)
    running = jnp.sum(arrived, axis=0).astype(jnp.bfloat16).reshape(width // groups, width)
    hidden = jnp.dot(running, cycle_integral_tiles[0], preferred_element_type=jnp.float32).astype(jnp.bfloat16)
    hidden = jnp.pad(hidden, ((0, 0), (0, LANES - width)))
    spread = lax.all_to_all(
        jnp.broadcast_to(hidden[None], (groups * tiles,) + hidden.shape), ALL, split_axis=0, concat_axis=0, tiled=True
    )

    packed = pack_factors(ladder_factor[0])
    mine = lax.dynamic_index_in_dim(packed, core, 0, keepdims=False)
    halves = {0: mine}
    for up in range(1, tiles // across):
        halves[up * across] = to_tile(mine, up * across)
    for up in range(tiles // across):
        source = halves[up * across]
        if up * across >= tiles // 2:
            source, _ = lax.optimization_barrier((source, hidden))
            halves[up * across] = source
        for side in range(1, across):
            halves[up * across + side] = to_tile(source, side)

    blocks = jnp.pad(block_list.reshape(rows, width, width), ((0, 0), (0, LANES - width), (0, LANES - width)))
    place = me.reshape(1)
    total = ladder((0,), names, place, blocks, None, [packed[0], packed[1]], tiles, width, pairs)
    for near in (tuple(range(1, tiles // 2)), tuple(range(tiles // 2, tiles))):
        parts = []
        for slot in near:
            parts += [halves[slot], to_core(halves[slot])]
        total, *parts = lax.optimization_barrier((total, *parts))
        total = ladder(near, names, place, blocks, total, parts, tiles, width, pairs)
    residual = close(names, blocks, total, spread, tiles, width)
    return residual.reshape(pairs, slots, flat)


def solution(mesh):
    in_specs = (
        P(("grp", "tile"), None, None),
        P(("grp", "tile"), None),
        P(("grp", "tile")),
        P("tile", None, None, None),
        P("tile", None, None),
    )
    out_specs = P(("grp", "tile"), None, None)
    return jax.shard_map(
        on_device, mesh=mesh, in_specs=in_specs, out_specs=out_specs, check_vma=False
    )
```

```python
import functools

import jax
import jax.numpy as jnp
from jax import lax
from jax.experimental import pallas as pl
from jax.experimental.pallas import tpu as pltpu
from jax.sharding import PartitionSpec as P

LANES = 128
ALL = ("grp", "tile")


def pack_factors(factors):
    count, width, _ = factors.shape
    quads = factors.reshape(count // 4, 4, width, width)
    spare = LANES - width
    pieces = [quads[:, 3, :, i * spare:(i + 1) * spare] for i in range(3)]
    packed = jnp.concatenate([quads[:, :3], jnp.stack(pieces, axis=1)], axis=-1)
    return packed.reshape(2, count // 8 * 3, width, LANES)


def unpack(refs, stacked, beside, width):
    spare = LANES - width
    lane = lax.broadcasted_iota(jnp.int32, (width, LANES), 1)
    number = 0
    for ref in refs:
        for quad in range(ref.shape[0] // 3):
            parts = [ref[quad * 3 + i] for i in range(3)]
            wide = [part.astype(jnp.float32) for part in parts]
            moved = [pltpu.roll(wide[i], spare * (i + 1), 1) for i in range(3)]
            fourth = jnp.where(lane < spare, moved[0], jnp.where(lane < 2 * spare, moved[1], moved[2]))
            parts.append(fourth.astype(jnp.bfloat16))
            for part in parts:
                stacked[number * width:(number + 1) * width, :] = part
                beside[:, number * LANES:(number + 1) * LANES] = part
                number += 1


def ladder_kernel(near, tiles, width, carried, kept_ref, me_ref, blocks_ref, *rest):
    rest = rest[carried:]
    factor_refs, total_ref = rest[:2 * len(near)], rest[2 * len(near)]
    table, counts, jobs, landed, stacked, beside, grown, sems = rest[2 * len(near) + 1:]
    rows = blocks_ref.shape[0]
    most = table.shape[0] // tiles
    me = me_ref[0]
    copies = [pltpu.make_async_copy(ref, landed.at[i], sems.at[i]) for i, ref in enumerate(factor_refs)]
    for copy in copies:
        copy.start()

    def clear(j, _):
        counts[j] = 0
        return 0

    lax.fori_loop(0, tiles, clear, 0)

    def fill(r, _):
        slot = kept_ref[r] ^ me
        n = counts[slot]
        table[slot * most + n] = r
        counts[slot] = n + 1
        return 0

    lax.fori_loop(0, rows, fill, 0)

    last = jnp.int32(0)
    for number, slot in enumerate(near):
        count = counts[slot]

        def add(i, at, number=number, slot=slot, count=count):
            jobs[3 * at] = number
            jobs[3 * at + 1] = table[slot * most + 2 * i]
            jobs[3 * at + 2] = table[slot * most + jnp.minimum(2 * i + 1, count - 1)]
            return at + 1

        last = lax.fori_loop(0, (count + 1) // 2, add, last)
    for number in range(len(near)):
        copies[2 * number].wait()
        copies[2 * number + 1].wait()
        unpack((landed.at[2 * number], landed.at[2 * number + 1]), stacked.at[number], beside.at[number], width)

    factor_count = stacked.shape[1] // width
    step = 4

    def grow(at, side):
        number = jobs[3 * at]
        pair = jnp.concatenate([blocks_ref[jobs[3 * at + 1]], blocks_ref[jobs[3 * at + 2]]], axis=1)
        for q in range(0, factor_count, step):
            inner = jnp.dot(
                stacked[number, q * width:(q + step) * width], pair, preferred_element_type=jnp.float32
            ).astype(jnp.bfloat16)
            for f in range(step):
                part, lanes = inner[f * width:(f + 1) * width], slice((q + f) * LANES, (q + f + 1) * LANES)
                grown[side, 0:width, lanes] = part[:, :LANES]
                grown[side, width:2 * width, lanes] = part[:, LANES:]

    def reduce(at, side):
        total = lax.dot_general(
            grown[side], beside[jobs[3 * at]], (((1,), (1,)), ((), ())), preferred_element_type=jnp.float32
        )
        total_ref[jobs[3 * at + 1]] = total[:width]
        total_ref[jobs[3 * at + 2]] = total[width:]

    def two(i, _):
        first, second = 2 * i, jnp.minimum(2 * i + 1, last - 1)
        grow(first, 0)
        grow(second, 1)
        reduce(first, 0)
        reduce(second, 1)
        return 0

    lax.fori_loop(0, (last + 1) // 2, two, 0)


SMEM, VMEM = pl.BlockSpec(memory_space=pltpu.SMEM), pl.BlockSpec(memory_space=pltpu.VMEM)
FREE = pl.BlockSpec(memory_space=pl.ANY)


def ladder(near, kept, me, blocks, total, parts, tiles, width, most, cost):
    rows = blocks.shape[0]
    factor_count = parts[0].shape[0] // 3 * 4 * 2
    carried = [] if total is None else [total]
    return pl.pallas_call(
        functools.partial(ladder_kernel, near, tiles, width, len(carried)),
        out_shape=jax.ShapeDtypeStruct((rows, width, width), jnp.float32),
        in_specs=[SMEM, SMEM] + [VMEM] * (1 + len(carried)) + [FREE] * len(parts),
        out_specs=VMEM,
        input_output_aliases={} if total is None else {3: 0},
        scratch_shapes=[
            pltpu.SMEM((tiles * most,), jnp.int32),
            pltpu.SMEM((tiles,), jnp.int32),
            pltpu.SMEM((3 * (rows + tiles),), jnp.int32),
            pltpu.VMEM((len(parts),) + parts[0].shape, jnp.bfloat16),
            pltpu.VMEM((len(near), factor_count * width, LANES), jnp.bfloat16),
            pltpu.VMEM((len(near), width, factor_count * LANES), jnp.bfloat16),
            pltpu.VMEM((2, 2 * width, factor_count * LANES), jnp.bfloat16),
            pltpu.SemaphoreType.DMA((len(parts),)),
        ],
        compiler_params=pltpu.CompilerParams(vmem_limit_bytes=(10 << 20) + (len(near) << 21)),
        cost_estimate=pl.CostEstimate(flops=cost, bytes_accessed=rows, transcendentals=0),
    )(kept, me, blocks, *carried, *parts)


def close_kernel(tiles, width, kept_ref, blocks_ref, total_ref, spread_ref, out_ref, landed, hidden, sem):
    groups = spread_ref.shape[0] // tiles
    copy = pltpu.make_async_copy(spread_ref, landed, sem)
    copy.start()
    hidden[:, width:, :] = jnp.zeros((tiles, LANES - width, LANES), jnp.bfloat16)
    copy.wait()
    for tile in range(tiles):
        pieces = [landed[g * tiles + tile].astype(jnp.float32) for g in range(groups)]
        hidden[tile, :width, :] = jnp.concatenate(pieces, axis=0).astype(jnp.bfloat16)
    for r in range(blocks_ref.shape[0]):
        term = jnp.dot(blocks_ref[r, :width, :], hidden[kept_ref[r]], preferred_element_type=jnp.float32)
        out_ref[r] = (total_ref[r] + term[:, :width]).astype(jnp.bfloat16)


def close(kept, blocks, total, spread, tiles, width):
    rows = blocks.shape[0]
    return pl.pallas_call(
        functools.partial(close_kernel, tiles, width),
        out_shape=jax.ShapeDtypeStruct((rows, width, width), jnp.bfloat16),
        in_specs=[SMEM] + [VMEM] * 2 + [FREE],
        out_specs=VMEM,
        scratch_shapes=[
            pltpu.VMEM(spread.shape, jnp.bfloat16),
            pltpu.VMEM((tiles, LANES, LANES), jnp.bfloat16),
            pltpu.SemaphoreType.DMA,
        ],
        compiler_params=pltpu.CompilerParams(vmem_limit_bytes=16 << 20),
        cost_estimate=pl.CostEstimate(flops=rows, bytes_accessed=rows, transcendentals=0),
    )(kept, blocks, total, spread)


def on_device(amplitudes, kept, coef, ladder_factor, cycle_integral_tiles):
    pairs, slots, flat = amplitudes.shape
    width = ladder_factor.shape[-1]
    tiles, groups = lax.axis_size("tile"), lax.axis_size("grp")
    across = 1 << ((tiles.bit_length() - 1) // 2)
    rows = pairs * slots
    me = lax.axis_index("tile")
    core = lax.axis_index("grp") % 2

    def to_tile(array, flip):
        return lax.ppermute(array, "tile", [(i, i ^ flip) for i in range(tiles)])

    def to_core(array):
        return lax.ppermute(array, "grp", [(i, i ^ 1) for i in range(groups)])

    block_list = amplitudes.reshape(rows, flat)
    names = kept.reshape(rows)
    weights = jnp.where(
        jnp.arange(tiles, dtype=jnp.int32)[:, None] == names[None, :], jnp.repeat(coef, slots)[None, :], jnp.zeros((), coef.dtype)
    )
    part_sum = jnp.dot(weights, block_list, preferred_element_type=jnp.float32)
    share = flat // groups
    shares = part_sum.reshape(tiles, groups, share).transpose(1, 0, 2).reshape(groups * tiles, share)
    arrived = lax.all_to_all(shares, ALL, split_axis=0, concat_axis=0, tiled=True)
    running = jnp.sum(arrived, axis=0).astype(jnp.bfloat16).reshape(width // groups, width)
    hidden = jnp.dot(running, cycle_integral_tiles[0], preferred_element_type=jnp.float32).astype(jnp.bfloat16)
    hidden = jnp.pad(hidden, ((0, 0), (0, LANES - width)))
    spread = lax.all_to_all(
        jnp.broadcast_to(hidden[None], (groups * tiles,) + hidden.shape), ALL, split_axis=0, concat_axis=0, tiled=True
    )

    blocks = jnp.pad(block_list.reshape(rows, width, width), ((0, 0), (0, LANES - width), (0, LANES - width)))
    place = me.reshape(1)
    packed = pack_factors(ladder_factor[0])
    mine = lax.dynamic_index_in_dim(packed, core, 0, keepdims=False)
    half = tiles // 2
    halves = {0: mine}
    for up in range(across, tiles, across):
        halves[up] = to_tile(mine, up)
    total = ladder((0,), names, place, blocks, None, [packed[0], packed[1]], tiles, width, pairs, rows)

    def cross(starts, gate):
        for up in starts:
            source = halves[up]
            if up:
                source, _ = lax.optimization_barrier((source, gate))
                halves[up] = source
            for side in range(1, across):
                halves[up + side] = to_tile(source, side)

    def stage(near, total, gate, cost):
        parts = []
        for slot in near:
            parts += [halves[slot], to_core(halves[slot])]
        total, _, *parts = lax.optimization_barrier((total, gate, *parts))
        return ladder(near, names, place, blocks, total, parts, tiles, width, pairs, cost)

    cross(range(0, half, across), total)
    early = tuple(range(1, across + 1))
    total = stage(early, total, hidden, 30 * 10**9)
    cross(range(half, tiles, across), total)
    total = stage(tuple(s for s in range(1, tiles) if s not in early), total, total, rows)
    residual = close(names, blocks, total, spread, tiles, width)
    return residual.reshape(pairs, slots, flat)


def solution(mesh):
    in_specs = (
        P(("grp", "tile"), None, None),
        P(("grp", "tile"), None),
        P(("grp", "tile")),
        P("tile", None, None, None),
        P("tile", None, None),
    )
    out_specs = P(("grp", "tile"), None, None)
    return jax.shard_map(
        on_device, mesh=mesh, in_specs=in_specs, out_specs=out_specs, check_vma=False
    )
```

```python
import functools

import jax
import jax.numpy as jnp
from jax import lax
from jax.experimental import pallas as pl
from jax.experimental.pallas import tpu as pltpu
from jax.sharding import PartitionSpec as P

LANES = 128
ALL = ("grp", "tile")


def pack_factors(factors):
    count, width, _ = factors.shape
    quads = factors.reshape(count // 4, 4, width, width)
    spare = LANES - width
    pieces = [quads[:, 3, :, i * spare:(i + 1) * spare] for i in range(3)]
    packed = jnp.concatenate([quads[:, :3], jnp.stack(pieces, axis=1)], axis=-1)
    return packed.reshape(2, count // 8 * 3, width, LANES)


def unpack(refs, stacked, beside, width):
    spare = LANES - width
    lane = lax.broadcasted_iota(jnp.int32, (width, LANES), 1)
    number = 0
    for ref in refs:
        for quad in range(ref.shape[0] // 3):
            parts = [ref[quad * 3 + i] for i in range(3)]
            wide = [part.astype(jnp.float32) for part in parts]
            moved = [pltpu.roll(wide[i], spare * (i + 1), 1) for i in range(3)]
            fourth = jnp.where(lane < spare, moved[0], jnp.where(lane < 2 * spare, moved[1], moved[2]))
            parts.append(fourth.astype(jnp.bfloat16))
            for part in parts:
                stacked[number * width:(number + 1) * width, :] = part
                beside[:, number * LANES:(number + 1) * LANES] = part
                number += 1


def ladder_kernel(near, tiles, width, carried, kept_ref, me_ref, blocks_ref, *rest):
    rest = rest[carried:]
    factor_refs, total_ref = rest[:2 * len(near)], rest[2 * len(near)]
    table, counts, jobs, landed, stacked, beside, grown, sems = rest[2 * len(near) + 1:]
    rows = blocks_ref.shape[0]
    most = table.shape[0] // tiles
    me = me_ref[0]
    copies = [pltpu.make_async_copy(ref, landed.at[i], sems.at[i]) for i, ref in enumerate(factor_refs)]
    for copy in copies:
        copy.start()

    def clear(j, _):
        counts[j] = 0
        return 0

    lax.fori_loop(0, tiles, clear, 0)

    def fill(r, _):
        slot = kept_ref[r] ^ me
        n = counts[slot]
        table[slot * most + n] = r
        counts[slot] = n + 1
        return 0

    lax.fori_loop(0, rows, fill, 0)

    last = jnp.int32(0)
    for number, slot in enumerate(near):
        count = counts[slot]

        def add(i, at, number=number, slot=slot, count=count):
            jobs[3 * at] = number
            jobs[3 * at + 1] = table[slot * most + 2 * i]
            jobs[3 * at + 2] = table[slot * most + jnp.minimum(2 * i + 1, count - 1)]
            return at + 1

        last = lax.fori_loop(0, (count + 1) // 2, add, last)
    for number in range(len(near)):
        copies[2 * number].wait()
        copies[2 * number + 1].wait()
        unpack((landed.at[2 * number], landed.at[2 * number + 1]), stacked.at[number], beside.at[number], width)

    factor_count = stacked.shape[1] // width
    step = 4

    def grow(at, side):
        number = jobs[3 * at]
        pair = jnp.concatenate([blocks_ref[jobs[3 * at + 1]], blocks_ref[jobs[3 * at + 2]]], axis=1)
        for q in range(0, factor_count, step):
            inner = jnp.dot(
                stacked[number, q * width:(q + step) * width], pair, preferred_element_type=jnp.float32
            ).astype(jnp.bfloat16)
            for f in range(step):
                part, lanes = inner[f * width:(f + 1) * width], slice((q + f) * LANES, (q + f + 1) * LANES)
                grown[side, 0:width, lanes] = part[:, :LANES]
                grown[side, width:2 * width, lanes] = part[:, LANES:]

    def reduce(at, side):
        total = lax.dot_general(
            grown[side], beside[jobs[3 * at]], (((1,), (1,)), ((), ())), preferred_element_type=jnp.float32
        )
        total_ref[jobs[3 * at + 1]] = total[:width]
        total_ref[jobs[3 * at + 2]] = total[width:]

    def two(i, _):
        first, second = 2 * i, jnp.minimum(2 * i + 1, last - 1)
        grow(first, 0)
        grow(second, 1)
        reduce(first, 0)
        reduce(second, 1)
        return 0

    lax.fori_loop(0, (last + 1) // 2, two, 0)


SMEM, VMEM = pl.BlockSpec(memory_space=pltpu.SMEM), pl.BlockSpec(memory_space=pltpu.VMEM)
FREE = pl.BlockSpec(memory_space=pl.ANY)


def ladder(near, kept, me, blocks, total, parts, tiles, width, most, cost):
    rows = blocks.shape[0]
    factor_count = parts[0].shape[0] // 3 * 4 * 2
    carried = [] if total is None else [total]
    return pl.pallas_call(
        functools.partial(ladder_kernel, near, tiles, width, len(carried)),
        out_shape=jax.ShapeDtypeStruct((rows, width, width), jnp.float32),
        in_specs=[SMEM, SMEM] + [VMEM] * (1 + len(carried)) + [FREE] * len(parts),
        out_specs=VMEM,
        input_output_aliases={} if total is None else {3: 0},
        scratch_shapes=[
            pltpu.SMEM((tiles * most,), jnp.int32),
            pltpu.SMEM((tiles,), jnp.int32),
            pltpu.SMEM((3 * (rows + tiles),), jnp.int32),
            pltpu.VMEM((len(parts),) + parts[0].shape, jnp.bfloat16),
            pltpu.VMEM((len(near), factor_count * width, LANES), jnp.bfloat16),
            pltpu.VMEM((len(near), width, factor_count * LANES), jnp.bfloat16),
            pltpu.VMEM((2, 2 * width, factor_count * LANES), jnp.bfloat16),
            pltpu.SemaphoreType.DMA((len(parts),)),
        ],
        compiler_params=pltpu.CompilerParams(vmem_limit_bytes=(10 << 20) + (len(near) << 21)),
        cost_estimate=pl.CostEstimate(flops=cost, bytes_accessed=rows, transcendentals=0),
    )(kept, me, blocks, *carried, *parts)


def close_kernel(tiles, width, kept_ref, blocks_ref, total_ref, spread_ref, out_ref, landed, hidden, sem):
    groups = spread_ref.shape[0] // tiles
    copy = pltpu.make_async_copy(spread_ref, landed, sem)
    copy.start()
    hidden[:, width:, :] = jnp.zeros((tiles, LANES - width, LANES), jnp.bfloat16)
    copy.wait()
    for tile in range(tiles):
        pieces = [landed[g * tiles + tile].astype(jnp.float32) for g in range(groups)]
        hidden[tile, :width, :] = jnp.concatenate(pieces, axis=0).astype(jnp.bfloat16)
    for r in range(blocks_ref.shape[0]):
        term = jnp.dot(blocks_ref[r, :width, :], hidden[kept_ref[r]], preferred_element_type=jnp.float32)
        out_ref[r] = (total_ref[r] + term[:, :width]).astype(jnp.bfloat16)


def close(kept, blocks, total, spread, tiles, width):
    rows = blocks.shape[0]
    return pl.pallas_call(
        functools.partial(close_kernel, tiles, width),
        out_shape=jax.ShapeDtypeStruct((rows, width, width), jnp.bfloat16),
        in_specs=[SMEM] + [VMEM] * 2 + [FREE],
        out_specs=VMEM,
        scratch_shapes=[
            pltpu.VMEM(spread.shape, jnp.bfloat16),
            pltpu.VMEM((tiles, LANES, LANES), jnp.bfloat16),
            pltpu.SemaphoreType.DMA,
        ],
        compiler_params=pltpu.CompilerParams(vmem_limit_bytes=16 << 20),
        cost_estimate=pl.CostEstimate(flops=rows, bytes_accessed=rows, transcendentals=0),
    )(kept, blocks, total, spread)


def on_device(amplitudes, kept, coef, ladder_factor, cycle_integral_tiles):
    pairs, slots, flat = amplitudes.shape
    width = ladder_factor.shape[-1]
    tiles, groups = lax.axis_size("tile"), lax.axis_size("grp")
    across = 1 << ((tiles.bit_length() - 1) // 2)
    rows = pairs * slots
    me = lax.axis_index("tile")
    core = lax.axis_index("grp") % 2

    def to_tile(array, flip):
        return lax.ppermute(array, "tile", [(i, i ^ flip) for i in range(tiles)])

    def to_core(array):
        return lax.ppermute(array, "grp", [(i, i ^ 1) for i in range(groups)])

    block_list = amplitudes.reshape(rows, flat)
    names = kept.reshape(rows)
    weights = jnp.where(
        jnp.arange(tiles, dtype=jnp.int32)[:, None] == names[None, :], jnp.repeat(coef, slots)[None, :], jnp.zeros((), coef.dtype)
    )
    part_sum = jnp.dot(weights, block_list, preferred_element_type=jnp.float32)
    share = flat // groups
    shares = part_sum.reshape(tiles, groups, share).transpose(1, 0, 2).reshape(groups * tiles, share)
    arrived = lax.all_to_all(shares, ALL, split_axis=0, concat_axis=0, tiled=True)
    blocks = jnp.pad(block_list.reshape(rows, width, width), ((0, 0), (0, LANES - width), (0, LANES - width)))
    place = me.reshape(1)
    packed = pack_factors(ladder_factor[0])
    mine = lax.dynamic_index_in_dim(packed, core, 0, keepdims=False)
    half = tiles // 2
    halves = {0: mine}
    for up in range(across, tiles, across):
        halves[up] = to_tile(mine, up)
    total = ladder((0,), names, place, blocks, None, [packed[0], packed[1]], tiles, width, pairs, rows)

    def cross(starts, gate):
        for up in starts:
            source = halves[up]
            if up:
                source, _ = lax.optimization_barrier((source, gate))
                halves[up] = source
            for side in range(1, across):
                halves[up + side] = to_tile(source, side)

    def stage(near, total, gate, cost):
        parts = []
        for slot in near:
            parts += [halves[slot], to_core(halves[slot])]
        total, _, *parts = lax.optimization_barrier((total, gate, *parts))
        return ladder(near, names, place, blocks, total, parts, tiles, width, pairs, cost)

    cross(range(0, half, across), total)
    cross(range(half, tiles, across), total)
    arrived, _ = lax.optimization_barrier((arrived, total))
    running = jnp.sum(arrived, axis=0).astype(jnp.bfloat16).reshape(width // groups, width)
    hidden = jnp.dot(running, cycle_integral_tiles[0], preferred_element_type=jnp.float32).astype(jnp.bfloat16)
    hidden = jnp.pad(hidden, ((0, 0), (0, LANES - width)))
    spread = lax.all_to_all(
        jnp.broadcast_to(hidden[None], (groups * tiles,) + hidden.shape), ALL, split_axis=0, concat_axis=0, tiled=True
    )

    early = tuple(range(1, across + 1))
    last = tuple(range(half, half + across))
    middle = tuple(s for s in range(1, tiles) if s not in early + last)
    total = stage(early, total, total, rows)
    for slot in middle + last:
        halves[slot], _ = lax.optimization_barrier((halves[slot], total))
    total = stage(middle, total, total, rows)
    total = stage(last, total, total, rows)
    residual = close(names, blocks, total, spread, tiles, width)
    return residual.reshape(pairs, slots, flat)


def solution(mesh):
    in_specs = (
        P(("grp", "tile"), None, None),
        P(("grp", "tile"), None),
        P(("grp", "tile")),
        P("tile", None, None, None),
        P("tile", None, None),
    )
    out_specs = P(("grp", "tile"), None, None)
    return jax.shard_map(
        on_device, mesh=mesh, in_specs=in_specs, out_specs=out_specs, check_vma=False
    )
```

```python
import functools

import jax
import jax.numpy as jnp
from jax import lax
from jax.experimental import pallas as pl
from jax.experimental.pallas import tpu as pltpu
from jax.sharding import PartitionSpec as P

LANES = 128
ALL = ("grp", "tile")


def pack_factors(factors):
    count, width, _ = factors.shape
    quads = factors.reshape(count // 4, 4, width, width)
    spare = LANES - width
    pieces = [quads[:, 3, :, i * spare:(i + 1) * spare] for i in range(3)]
    packed = jnp.concatenate([quads[:, :3], jnp.stack(pieces, axis=1)], axis=-1)
    return packed.reshape(2, count // 8 * 3, width, LANES)


def unpack(refs, stacked, beside, width):
    spare = LANES - width
    lane = lax.broadcasted_iota(jnp.int32, (width, LANES), 1)
    number = 0
    for ref in refs:
        for quad in range(ref.shape[0] // 3):
            parts = [ref[quad * 3 + i] for i in range(3)]
            wide = [part.astype(jnp.float32) for part in parts]
            moved = [pltpu.roll(wide[i], spare * (i + 1), 1) for i in range(3)]
            fourth = jnp.where(lane < spare, moved[0], jnp.where(lane < 2 * spare, moved[1], moved[2]))
            parts.append(fourth.astype(jnp.bfloat16))
            for part in parts:
                stacked[number * width:(number + 1) * width, :] = part
                beside[:, number * LANES:(number + 1) * LANES] = part
                number += 1


def ladder_kernel(near, tiles, width, carried, kept_ref, me_ref, blocks_ref, *rest):
    rest = rest[carried:]
    factor_refs, total_ref = rest[:2 * len(near)], rest[2 * len(near)]
    table, counts, jobs, landed, stacked, beside, grown, sems = rest[2 * len(near) + 1:]
    rows = blocks_ref.shape[0]
    most = table.shape[0] // tiles
    me = me_ref[0]
    copies = [pltpu.make_async_copy(ref, landed.at[i], sems.at[i]) for i, ref in enumerate(factor_refs)]
    for copy in copies:
        copy.start()

    def clear(j, _):
        counts[j] = 0
        return 0

    lax.fori_loop(0, tiles, clear, 0)

    def fill(r, _):
        slot = kept_ref[r] ^ me
        n = counts[slot]
        table[slot * most + n] = r
        counts[slot] = n + 1
        return 0

    lax.fori_loop(0, rows, fill, 0)

    last = jnp.int32(0)
    for number, slot in enumerate(near):
        count = counts[slot]

        def add(i, at, number=number, slot=slot, count=count):
            jobs[3 * at] = number
            jobs[3 * at + 1] = table[slot * most + 2 * i]
            jobs[3 * at + 2] = table[slot * most + jnp.minimum(2 * i + 1, count - 1)]
            return at + 1

        last = lax.fori_loop(0, (count + 1) // 2, add, last)
    for number in range(len(near)):
        copies[2 * number].wait()
        copies[2 * number + 1].wait()
        unpack((landed.at[2 * number], landed.at[2 * number + 1]), stacked.at[number], beside.at[number], width)

    factor_count = stacked.shape[1] // width
    step = 4

    def grow(at, side):
        number = jobs[3 * at]
        pair = jnp.concatenate([blocks_ref[jobs[3 * at + 1]], blocks_ref[jobs[3 * at + 2]]], axis=1)
        for q in range(0, factor_count, step):
            inner = jnp.dot(
                stacked[number, q * width:(q + step) * width], pair, preferred_element_type=jnp.float32
            ).astype(jnp.bfloat16)
            for f in range(step):
                part, lanes = inner[f * width:(f + 1) * width], slice((q + f) * LANES, (q + f + 1) * LANES)
                grown[side, 0:width, lanes] = part[:, :LANES]
                grown[side, width:2 * width, lanes] = part[:, LANES:]

    def reduce(at, side):
        total = lax.dot_general(
            grown[side], beside[jobs[3 * at]], (((1,), (1,)), ((), ())), preferred_element_type=jnp.float32
        )
        total_ref[jobs[3 * at + 1]] = total[:width]
        total_ref[jobs[3 * at + 2]] = total[width:]

    def two(i, _):
        first, second = 2 * i, jnp.minimum(2 * i + 1, last - 1)
        grow(first, 0)
        grow(second, 1)
        reduce(first, 0)
        reduce(second, 1)
        return 0

    lax.fori_loop(0, (last + 1) // 2, two, 0)


SMEM, VMEM = pl.BlockSpec(memory_space=pltpu.SMEM), pl.BlockSpec(memory_space=pltpu.VMEM)
FREE = pl.BlockSpec(memory_space=pl.ANY)


def ladder(near, kept, me, blocks, total, parts, tiles, width, most, cost):
    rows = blocks.shape[0]
    factor_count = parts[0].shape[0] // 3 * 4 * 2
    carried = [] if total is None else [total]
    return pl.pallas_call(
        functools.partial(ladder_kernel, near, tiles, width, len(carried)),
        out_shape=jax.ShapeDtypeStruct((rows, width, width), jnp.float32),
        in_specs=[SMEM, SMEM] + [VMEM] * (1 + len(carried)) + [FREE] * len(parts),
        out_specs=VMEM,
        input_output_aliases={} if total is None else {3: 0},
        scratch_shapes=[
            pltpu.SMEM((tiles * most,), jnp.int32),
            pltpu.SMEM((tiles,), jnp.int32),
            pltpu.SMEM((3 * (rows + tiles),), jnp.int32),
            pltpu.VMEM((len(parts),) + parts[0].shape, jnp.bfloat16),
            pltpu.VMEM((len(near), factor_count * width, LANES), jnp.bfloat16),
            pltpu.VMEM((len(near), width, factor_count * LANES), jnp.bfloat16),
            pltpu.VMEM((2, 2 * width, factor_count * LANES), jnp.bfloat16),
            pltpu.SemaphoreType.DMA((len(parts),)),
        ],
        compiler_params=pltpu.CompilerParams(vmem_limit_bytes=(10 << 20) + (len(near) << 21)),
        cost_estimate=pl.CostEstimate(flops=cost, bytes_accessed=rows, transcendentals=0),
    )(kept, me, blocks, *carried, *parts)


def close_kernel(tiles, width, kept_ref, blocks_ref, total_ref, spread_ref, out_ref, landed, hidden, square, lines, sem):
    groups = spread_ref.shape[0] // tiles
    pairs, slots, flat = out_ref.shape
    count = flat // LANES
    parts = width * 4 // LANES
    copy = pltpu.make_async_copy(spread_ref, landed, sem)
    copy.start()
    hidden[:, width:, :] = jnp.zeros((tiles, LANES - width, LANES), jnp.bfloat16)
    copy.wait()
    for tile in range(tiles):
        pieces = [landed[g * tiles + tile].astype(jnp.float32) for g in range(groups)]
        hidden[tile, :width, :] = jnp.concatenate(pieces, axis=0).astype(jnp.bfloat16)
    spare = LANES - width
    lane = lax.broadcasted_iota(jnp.int32, (width // 4, LANES), 1)
    for pair in range(pairs):
        for slot in range(slots):
            r = pair * slots + slot
            term = jnp.dot(blocks_ref[r, :width, :], hidden[kept_ref[r]], preferred_element_type=jnp.float32)
            square[r, :, :width] = total_ref[r] + term[:, :width]
            quarter = [square[r, pl.ds(j, width // 4, stride=4), :] for j in range(4)]
            second = pltpu.roll(quarter[1], width, 1)
            third = pltpu.roll(quarter[2], 2 * spare, 1)
            fourth = pltpu.roll(quarter[3], spare, 1)
            packed = (
                jnp.where(lane < width, quarter[0], second),
                jnp.where(lane < 2 * spare, second, third),
                jnp.where(lane < spare, third, fourth),
            )
            for i in range(parts):
                lines[pair, pl.ds(slot * count + i, width // 4, stride=parts), :] = packed[i]
        for t in range(count):
            out_ref[pair, :, t * LANES:(t + 1) * LANES] = lines[pair, pl.ds(t, slots, stride=count), :].astype(jnp.bfloat16)


def close(kept, blocks, total, spread, tiles, width, shape):
    rows = blocks.shape[0]
    return pl.pallas_call(
        functools.partial(close_kernel, tiles, width),
        out_shape=jax.ShapeDtypeStruct(shape, jnp.bfloat16),
        in_specs=[SMEM] + [VMEM] * 2 + [FREE],
        out_specs=VMEM,
        scratch_shapes=[
            pltpu.VMEM(spread.shape, jnp.bfloat16),
            pltpu.VMEM((tiles, LANES, LANES), jnp.bfloat16),
            pltpu.VMEM((rows, width, LANES), jnp.float32),
            pltpu.VMEM((shape[0], shape[1] * shape[2] // LANES, LANES), jnp.float32),
            pltpu.SemaphoreType.DMA,
        ],
        compiler_params=pltpu.CompilerParams(vmem_limit_bytes=16 << 20),
        cost_estimate=pl.CostEstimate(flops=rows, bytes_accessed=rows, transcendentals=0),
    )(kept, blocks, total, spread)


def on_device(amplitudes, kept, coef, ladder_factor, cycle_integral_tiles):
    pairs, slots, flat = amplitudes.shape
    width = ladder_factor.shape[-1]
    tiles, groups = lax.axis_size("tile"), lax.axis_size("grp")
    across = 1 << ((tiles.bit_length() - 1) // 2)
    rows = pairs * slots
    me = lax.axis_index("tile")
    core = lax.axis_index("grp") % 2

    def to_tile(array, flip):
        return lax.ppermute(array, "tile", [(i, i ^ flip) for i in range(tiles)])

    def to_core(array):
        return lax.ppermute(array, "grp", [(i, i ^ 1) for i in range(groups)])

    block_list = amplitudes.reshape(rows, flat)
    names = kept.reshape(rows)
    weights = jnp.where(
        jnp.arange(tiles, dtype=jnp.int32)[:, None] == names[None, :], jnp.repeat(coef, slots)[None, :], jnp.zeros((), coef.dtype)
    )
    part_sum = jnp.dot(weights, block_list, preferred_element_type=jnp.float32)
    share = flat // groups
    shares = part_sum.reshape(tiles, groups, share).transpose(1, 0, 2).reshape(groups * tiles, share)
    arrived = lax.all_to_all(shares, ALL, split_axis=0, concat_axis=0, tiled=True)
    blocks = jnp.pad(block_list.reshape(rows, width, width), ((0, 0), (0, LANES - width), (0, LANES - width)))
    place = me.reshape(1)
    packed = pack_factors(ladder_factor[0])
    mine = lax.dynamic_index_in_dim(packed, core, 0, keepdims=False)
    half = tiles // 2
    halves = {0: mine}
    for up in range(across, tiles, across):
        halves[up] = to_tile(mine, up)
    total = ladder((0,), names, place, blocks, None, [packed[0], packed[1]], tiles, width, pairs, rows)

    def cross(starts, gate):
        for up in starts:
            source = halves[up]
            if up:
                source, _ = lax.optimization_barrier((source, gate))
                halves[up] = source
            for side in range(1, across):
                halves[up + side] = to_tile(source, side)

    def stage(near, total, gate, cost):
        parts = []
        for slot in near:
            parts += [halves[slot], to_core(halves[slot])]
        total, _, *parts = lax.optimization_barrier((total, gate, *parts))
        return ladder(near, names, place, blocks, total, parts, tiles, width, pairs, cost)

    for slot in range(1, half):
        if slot % across:
            halves[slot] = to_tile(mine, slot)
    cross(range(half, tiles, across), total)
    arrived, _ = lax.optimization_barrier((arrived, total))
    running = jnp.sum(arrived, axis=0).astype(jnp.bfloat16).reshape(width // groups, width)
    hidden = jnp.dot(running, cycle_integral_tiles[0], preferred_element_type=jnp.float32).astype(jnp.bfloat16)
    hidden = jnp.pad(hidden, ((0, 0), (0, LANES - width)))
    spread = lax.all_to_all(
        jnp.broadcast_to(hidden[None], (groups * tiles,) + hidden.shape), ALL, split_axis=0, concat_axis=0, tiled=True
    )

    early = tuple(range(1, half))
    last = tuple(range(half, half + across))
    middle = tuple(s for s in range(1, tiles) if s not in early + last)
    total = stage(early, total, total, rows)
    for slot in middle + last:
        halves[slot], _ = lax.optimization_barrier((halves[slot], total))
    total = stage(middle, total, total, rows)
    total = stage(last, total, total, rows)
    return close(names, blocks, total, spread, tiles, width, amplitudes.shape)


def solution(mesh):
    in_specs = (
        P(("grp", "tile"), None, None),
        P(("grp", "tile"), None),
        P(("grp", "tile")),
        P("tile", None, None, None),
        P("tile", None, None),
    )
    out_specs = P(("grp", "tile"), None, None)
    return jax.shard_map(
        on_device, mesh=mesh, in_specs=in_specs, out_specs=out_specs, check_vma=False
    )
```

```python
import functools

import jax
import jax.numpy as jnp
from jax import lax
from jax.experimental import pallas as pl
from jax.experimental.pallas import tpu as pltpu
from jax.sharding import PartitionSpec as P

LANES = 128
ALL = ("grp", "tile")


def pack_factors(factors):
    count, width, _ = factors.shape
    quads = factors.reshape(count // 4, 4, width, width)
    spare = LANES - width
    pieces = [quads[:, 3, :, i * spare:(i + 1) * spare] for i in range(3)]
    packed = jnp.concatenate([quads[:, :3], jnp.stack(pieces, axis=1)], axis=-1)
    return packed.reshape(2, count // 8 * 3, width, LANES)


def unpack(refs, stacked, beside, width):
    spare = LANES - width
    lane = lax.broadcasted_iota(jnp.int32, (width, LANES), 1)
    number = 0
    for ref in refs:
        for quad in range(ref.shape[0] // 3):
            parts = [ref[quad * 3 + i] for i in range(3)]
            wide = [part.astype(jnp.float32) for part in parts]
            moved = [pltpu.roll(wide[i], spare * (i + 1), 1) for i in range(3)]
            fourth = jnp.where(lane < spare, moved[0], jnp.where(lane < 2 * spare, moved[1], moved[2]))
            parts.append(fourth.astype(jnp.bfloat16))
            for part in parts:
                stacked[number * width:(number + 1) * width, :] = part
                beside[:, number * LANES:(number + 1) * LANES] = part
                number += 1


def ladder_kernel(near, tiles, width, carried, kept_ref, me_ref, blocks_ref, *rest):
    rest = rest[carried:]
    factor_refs, total_ref = rest[:2 * len(near)], rest[2 * len(near)]
    table, counts, jobs, landed, stacked, beside, grown, sems = rest[2 * len(near) + 1:]
    rows = blocks_ref.shape[0]
    most = table.shape[0] // tiles
    me = me_ref[0]
    copies = [pltpu.make_async_copy(ref, landed.at[i], sems.at[i]) for i, ref in enumerate(factor_refs)]
    for copy in copies:
        copy.start()

    def clear(j, _):
        counts[j] = 0
        return 0

    lax.fori_loop(0, tiles, clear, 0)

    def fill(r, _):
        slot = kept_ref[r] ^ me
        n = counts[slot]
        table[slot * most + n] = r
        counts[slot] = n + 1
        return 0

    lax.fori_loop(0, rows, fill, 0)

    last = jnp.int32(0)
    for number, slot in enumerate(near):
        count = counts[slot]

        def add(i, at, number=number, slot=slot, count=count):
            jobs[3 * at] = number
            jobs[3 * at + 1] = table[slot * most + 2 * i]
            jobs[3 * at + 2] = table[slot * most + jnp.minimum(2 * i + 1, count - 1)]
            return at + 1

        last = lax.fori_loop(0, (count + 1) // 2, add, last)
    for number in range(len(near)):
        copies[2 * number].wait()
        copies[2 * number + 1].wait()
        unpack((landed.at[2 * number], landed.at[2 * number + 1]), stacked.at[number], beside.at[number], width)

    factor_count = stacked.shape[1] // width
    step = 4

    def grow(at, side):
        number = jobs[3 * at]
        pair = jnp.concatenate([blocks_ref[jobs[3 * at + 1]], blocks_ref[jobs[3 * at + 2]]], axis=1)
        for q in range(0, factor_count, step):
            inner = jnp.dot(
                stacked[number, q * width:(q + step) * width], pair, preferred_element_type=jnp.float32
            ).astype(jnp.bfloat16)
            for f in range(step):
                part, lanes = inner[f * width:(f + 1) * width], slice((q + f) * LANES, (q + f + 1) * LANES)
                grown[side, 0:width, lanes] = part[:, :LANES]
                grown[side, width:2 * width, lanes] = part[:, LANES:]

    def reduce(at, side):
        total = lax.dot_general(
            grown[side], beside[jobs[3 * at]], (((1,), (1,)), ((), ())), preferred_element_type=jnp.float32
        )
        total_ref[jobs[3 * at + 1]] = total[:width]
        total_ref[jobs[3 * at + 2]] = total[width:]

    def two(i, _):
        first, second = 2 * i, jnp.minimum(2 * i + 1, last - 1)
        grow(first, 0)
        grow(second, 1)
        reduce(first, 0)
        reduce(second, 1)
        return 0

    lax.fori_loop(0, (last + 1) // 2, two, 0)


SMEM, VMEM = pl.BlockSpec(memory_space=pltpu.SMEM), pl.BlockSpec(memory_space=pltpu.VMEM)
FREE = pl.BlockSpec(memory_space=pl.ANY)


def ladder(near, kept, me, blocks, total, parts, tiles, width, most, cost):
    rows = blocks.shape[0]
    factor_count = parts[0].shape[0] // 3 * 4 * 2
    carried = [] if total is None else [total]
    return pl.pallas_call(
        functools.partial(ladder_kernel, near, tiles, width, len(carried)),
        out_shape=jax.ShapeDtypeStruct((rows, width, width), jnp.float32),
        in_specs=[SMEM, SMEM] + [VMEM] * (1 + len(carried)) + [FREE] * len(parts),
        out_specs=VMEM,
        input_output_aliases={} if total is None else {3: 0},
        scratch_shapes=[
            pltpu.SMEM((tiles * most,), jnp.int32),
            pltpu.SMEM((tiles,), jnp.int32),
            pltpu.SMEM((3 * (rows + tiles),), jnp.int32),
            pltpu.VMEM((len(parts),) + parts[0].shape, jnp.bfloat16),
            pltpu.VMEM((len(near), factor_count * width, LANES), jnp.bfloat16),
            pltpu.VMEM((len(near), width, factor_count * LANES), jnp.bfloat16),
            pltpu.VMEM((2, 2 * width, factor_count * LANES), jnp.bfloat16),
            pltpu.SemaphoreType.DMA((len(parts),)),
        ],
        compiler_params=pltpu.CompilerParams(vmem_limit_bytes=(10 << 20) + (len(near) << 21)),
        cost_estimate=pl.CostEstimate(flops=cost, bytes_accessed=rows, transcendentals=0),
    )(kept, me, blocks, *carried, *parts)


def close_kernel(tiles, width, kept_ref, blocks_ref, total_ref, spread_ref, out_ref, landed, hidden, square, lines, sem):
    groups = spread_ref.shape[0] // tiles
    pairs, slots, flat = out_ref.shape
    count = flat // LANES
    parts = width * 4 // LANES
    copy = pltpu.make_async_copy(spread_ref, landed, sem)
    copy.start()
    hidden[:, width:, :] = jnp.zeros((tiles, LANES - width, LANES), jnp.bfloat16)
    copy.wait()
    for tile in range(tiles):
        pieces = [landed[g * tiles + tile].astype(jnp.float32) for g in range(groups)]
        hidden[tile, :width, :] = jnp.concatenate(pieces, axis=0).astype(jnp.bfloat16)
    spare = LANES - width
    lane = lax.broadcasted_iota(jnp.int32, (width // 4, LANES), 1)
    for pair in range(pairs):
        for slot in range(slots):
            r = pair * slots + slot
            term = jnp.dot(blocks_ref[r, :width, :], hidden[kept_ref[r]], preferred_element_type=jnp.float32)
            square[r, :, :width] = total_ref[r] + term[:, :width]
            quarter = [square[r, pl.ds(j, width // 4, stride=4), :] for j in range(4)]
            second = pltpu.roll(quarter[1], width, 1)
            third = pltpu.roll(quarter[2], 2 * spare, 1)
            fourth = pltpu.roll(quarter[3], spare, 1)
            packed = (
                jnp.where(lane < width, quarter[0], second),
                jnp.where(lane < 2 * spare, second, third),
                jnp.where(lane < spare, third, fourth),
            )
            for i in range(parts):
                lines[pair, pl.ds(slot * count + i, width // 4, stride=parts), :] = packed[i]
        for t in range(count):
            out_ref[pair, :, t * LANES:(t + 1) * LANES] = lines[pair, pl.ds(t, slots, stride=count), :].astype(jnp.bfloat16)


def close(kept, blocks, total, spread, tiles, width, shape):
    rows = blocks.shape[0]
    return pl.pallas_call(
        functools.partial(close_kernel, tiles, width),
        out_shape=jax.ShapeDtypeStruct(shape, jnp.bfloat16),
        in_specs=[SMEM] + [VMEM] * 2 + [FREE],
        out_specs=VMEM,
        scratch_shapes=[
            pltpu.VMEM(spread.shape, jnp.bfloat16),
            pltpu.VMEM((tiles, LANES, LANES), jnp.bfloat16),
            pltpu.VMEM((rows, width, LANES), jnp.float32),
            pltpu.VMEM((shape[0], shape[1] * shape[2] // LANES, LANES), jnp.float32),
            pltpu.SemaphoreType.DMA,
        ],
        compiler_params=pltpu.CompilerParams(vmem_limit_bytes=16 << 20),
        cost_estimate=pl.CostEstimate(flops=rows, bytes_accessed=rows, transcendentals=0),
    )(kept, blocks, total, spread)


def on_device(amplitudes, kept, coef, ladder_factor, cycle_integral_tiles):
    pairs, slots, flat = amplitudes.shape
    width = ladder_factor.shape[-1]
    tiles, groups = lax.axis_size("tile"), lax.axis_size("grp")
    across = 1 << ((tiles.bit_length() - 1) // 2)
    rows = pairs * slots
    me = lax.axis_index("tile")
    core = lax.axis_index("grp") % 2

    def to_tile(array, flip):
        return lax.ppermute(array, "tile", [(i, i ^ flip) for i in range(tiles)])

    def to_core(array):
        return lax.ppermute(array, "grp", [(i, i ^ 1) for i in range(groups)])

    block_list = amplitudes.reshape(rows, flat)
    names = kept.reshape(rows)
    weights = jnp.where(
        jnp.arange(tiles, dtype=jnp.int32)[:, None] == names[None, :], jnp.repeat(coef, slots)[None, :], jnp.zeros((), coef.dtype)
    )
    part_sum = jnp.dot(weights, block_list, preferred_element_type=jnp.float32)
    share = flat // groups
    shares = part_sum.reshape(tiles, groups, share).transpose(1, 0, 2).reshape(groups * tiles, share)
    blocks = jnp.pad(block_list.reshape(rows, width, width), ((0, 0), (0, LANES - width), (0, LANES - width)))
    place = me.reshape(1)
    packed = pack_factors(ladder_factor[0])
    mine = lax.dynamic_index_in_dim(packed, core, 0, keepdims=False)
    half = tiles // 2
    halves = {slot: to_tile(mine, slot) for slot in range(1, half)}
    shares, *_ = lax.optimization_barrier((shares, *halves.values()))
    arrived = lax.all_to_all(shares, ALL, split_axis=0, concat_axis=0, tiled=True)
    for up in range(half, tiles, across):
        halves[up] = to_tile(mine, up)

    def stage(near, total, cost):
        parts = []
        for slot in near:
            parts += [halves[slot], to_core(halves[slot])] if slot else [packed[0], packed[1]]
        return ladder(near, names, place, blocks, total, parts, tiles, width, pairs, cost)

    total = stage((0,), None, 1)
    first = total
    total = stage(tuple(range(1, half)), total, 1)
    arrived, _ = lax.optimization_barrier((arrived, total))
    running = jnp.sum(arrived, axis=0).astype(jnp.bfloat16).reshape(width // groups, width)
    hidden = jnp.dot(running, cycle_integral_tiles[0], preferred_element_type=jnp.float32).astype(jnp.bfloat16)
    hidden = jnp.pad(hidden, ((0, 0), (0, LANES - width)))
    spread = lax.all_to_all(
        jnp.broadcast_to(hidden[None], (groups * tiles,) + hidden.shape), ALL, split_axis=0, concat_axis=0, tiled=True
    )
    for up in range(half, tiles, across):
        halves[up], _ = lax.optimization_barrier((halves[up], total))
        for side in range(1, across):
            halves[up + side] = to_tile(halves[up], side)
    total = stage(tuple(range(half, tiles, across)), total, 1)
    total = stage(tuple(s for s in range(half, tiles) if s % across), total, 1)
    return close(names, blocks, total, spread, tiles, width, amplitudes.shape)


def solution(mesh):
    in_specs = (
        P(("grp", "tile"), None, None),
        P(("grp", "tile"), None),
        P(("grp", "tile")),
        P("tile", None, None, None),
        P("tile", None, None),
    )
    out_specs = P(("grp", "tile"), None, None)
    return jax.shard_map(
        on_device, mesh=mesh, in_specs=in_specs, out_specs=out_specs, check_vma=False
    )
```

```python
import functools

import jax
import jax.numpy as jnp
from jax import lax
from jax.experimental import pallas as pl
from jax.experimental.pallas import tpu as pltpu
from jax.sharding import PartitionSpec as P

LANES = 128
ALL = ("grp", "tile")


def pack_factors(factors):
    count, width, _ = factors.shape
    quads = factors.reshape(count // 4, 4, width, width)
    spare = LANES - width
    pieces = [quads[:, 3, :, i * spare:(i + 1) * spare] for i in range(3)]
    packed = jnp.concatenate([quads[:, :3], jnp.stack(pieces, axis=1)], axis=-1)
    return packed.reshape(2, count // 8 * 3, width, LANES)


def unpack(refs, stacked, beside, width):
    spare = LANES - width
    lane = lax.broadcasted_iota(jnp.int32, (width, LANES), 1)
    number = 0
    for ref in refs:
        for quad in range(ref.shape[0] // 3):
            parts = [ref[quad * 3 + i] for i in range(3)]
            wide = [part.astype(jnp.float32) for part in parts]
            moved = [pltpu.roll(wide[i], spare * (i + 1), 1) for i in range(3)]
            fourth = jnp.where(lane < spare, moved[0], jnp.where(lane < 2 * spare, moved[1], moved[2]))
            parts.append(fourth.astype(jnp.bfloat16))
            for part in parts:
                stacked[number * width:(number + 1) * width, :] = part
                beside[:, number * LANES:(number + 1) * LANES] = part
                number += 1


def ladder_kernel(near, tiles, width, carried, kept_ref, me_ref, blocks_ref, *rest):
    rest = rest[carried:]
    factor_refs, total_ref = rest[:2 * len(near)], rest[2 * len(near)]
    table, counts, jobs, stacked, beside, grown = rest[2 * len(near) + 1:]
    rows = blocks_ref.shape[0]
    most = table.shape[0] // tiles
    me = me_ref[0]
    slots = kept_ref.shape[0]
    for slot in range(tiles):
        counts[slot] = 0
    for r in range(rows):
        slot = kept_ref[r % slots, r // slots] ^ me
        n = counts[slot]
        table[slot * most + n] = r
        counts[slot] = n + 1

    last = jnp.int32(0)
    for number, slot in enumerate(near):
        count = counts[slot]

        def add(i, at, number=number, slot=slot, count=count):
            jobs[3 * at] = number
            jobs[3 * at + 1] = table[slot * most + 2 * i]
            jobs[3 * at + 2] = table[slot * most + jnp.minimum(2 * i + 1, count - 1)]
            return at + 1

        last = lax.fori_loop(0, (count + 1) // 2, add, last)
    for number in range(len(near)):
        unpack(factor_refs[2 * number:2 * number + 2], stacked.at[number], beside.at[number], width)

    factor_count = stacked.shape[1] // width
    step = 4

    def grow(at, side):
        number = jobs[3 * at]
        pair = jnp.concatenate([blocks_ref[jobs[3 * at + 1]], blocks_ref[jobs[3 * at + 2]]], axis=1)
        for q in range(0, factor_count, step):
            inner = jnp.dot(
                stacked[number, q * width:(q + step) * width], pair, preferred_element_type=jnp.float32
            ).astype(jnp.bfloat16)
            for f in range(step):
                part, lanes = inner[f * width:(f + 1) * width], slice((q + f) * LANES, (q + f + 1) * LANES)
                grown[side, 0:width, lanes] = part[:, :LANES]
                grown[side, width:2 * width, lanes] = part[:, LANES:]

    def reduce(at, side):
        total = lax.dot_general(
            grown[side], beside[jobs[3 * at]], (((1,), (1,)), ((), ())), preferred_element_type=jnp.float32
        )
        total_ref[jobs[3 * at + 1]] = total[:width]
        total_ref[jobs[3 * at + 2]] = total[width:]

    def two(i, _):
        first, second = 2 * i, jnp.minimum(2 * i + 1, last - 1)
        grow(first, 0)
        grow(second, 1)
        reduce(first, 0)
        reduce(second, 1)
        return 0

    lax.fori_loop(0, (last + 1) // 2, two, 0)


SMEM, VMEM = pl.BlockSpec(memory_space=pltpu.SMEM), pl.BlockSpec(memory_space=pltpu.VMEM)
FREE = pl.BlockSpec(memory_space=pl.ANY)


def ladder(near, kept, me, blocks, total, parts, tiles, width, most, cost):
    rows = blocks.shape[0]
    factor_count = parts[0].shape[0] // 3 * 4 * 2
    carried = [] if total is None else [total]
    return pl.pallas_call(
        functools.partial(ladder_kernel, near, tiles, width, len(carried)),
        out_shape=jax.ShapeDtypeStruct((rows, width, width), jnp.float32),
        in_specs=[SMEM, SMEM] + [VMEM] * (1 + len(carried)) + [VMEM] * len(parts),
        out_specs=VMEM,
        input_output_aliases={} if total is None else {3: 0},
        scratch_shapes=[
            pltpu.SMEM((tiles * most,), jnp.int32),
            pltpu.SMEM((tiles,), jnp.int32),
            pltpu.SMEM((3 * (rows + tiles),), jnp.int32),
            pltpu.VMEM((len(near), factor_count * width, LANES), jnp.bfloat16),
            pltpu.VMEM((len(near), width, factor_count * LANES), jnp.bfloat16),
            pltpu.VMEM((2, 2 * width, factor_count * LANES), jnp.bfloat16),
        ],
        compiler_params=pltpu.CompilerParams(vmem_limit_bytes=(10 << 20) + (len(near) << 21)),
        cost_estimate=pl.CostEstimate(flops=cost, bytes_accessed=rows, transcendentals=0),
    )(kept, me, blocks, *carried, *parts)


def close_kernel(tiles, width, kept_ref, blocks_ref, total_ref, spread_ref, out_ref, landed, hidden, square, lines, sem):
    groups = spread_ref.shape[0] // tiles
    pairs, slots, flat = out_ref.shape
    count = flat // LANES
    parts = width * 4 // LANES
    copy = pltpu.make_async_copy(spread_ref, landed, sem)
    copy.start()
    hidden[:, width:, :] = jnp.zeros((tiles, LANES - width, LANES), jnp.bfloat16)
    copy.wait()
    for tile in range(tiles):
        pieces = [landed[g * tiles + tile].astype(jnp.float32) for g in range(groups)]
        hidden[tile, :width, :] = jnp.concatenate(pieces, axis=0).astype(jnp.bfloat16)
    spare = LANES - width
    lane = lax.broadcasted_iota(jnp.int32, (width // 4, LANES), 1)
    for pair in range(pairs):
        for slot in range(slots):
            r = pair * slots + slot
            term = jnp.dot(blocks_ref[r, :width, :], hidden[kept_ref[slot, pair]], preferred_element_type=jnp.float32)
            square[r, :, :width] = total_ref[r] + term[:, :width]
            quarter = [square[r, pl.ds(j, width // 4, stride=4), :] for j in range(4)]
            second = pltpu.roll(quarter[1], width, 1)
            third = pltpu.roll(quarter[2], 2 * spare, 1)
            fourth = pltpu.roll(quarter[3], spare, 1)
            packed = (
                jnp.where(lane < width, quarter[0], second),
                jnp.where(lane < 2 * spare, second, third),
                jnp.where(lane < spare, third, fourth),
            )
            for i in range(parts):
                lines[pair, pl.ds(slot * count + i, width // 4, stride=parts), :] = packed[i]
        for t in range(count):
            out_ref[pair, :, t * LANES:(t + 1) * LANES] = lines[pair, pl.ds(t, slots, stride=count), :].astype(jnp.bfloat16)


def close(kept, blocks, total, spread, tiles, width, shape):
    rows = blocks.shape[0]
    return pl.pallas_call(
        functools.partial(close_kernel, tiles, width),
        out_shape=jax.ShapeDtypeStruct(shape, jnp.bfloat16),
        in_specs=[SMEM] + [VMEM] * 2 + [FREE],
        out_specs=VMEM,
        scratch_shapes=[
            pltpu.VMEM(spread.shape, jnp.bfloat16),
            pltpu.VMEM((tiles, LANES, LANES), jnp.bfloat16),
            pltpu.VMEM((rows, width, LANES), jnp.float32),
            pltpu.VMEM((shape[0], shape[1] * shape[2] // LANES, LANES), jnp.float32),
            pltpu.SemaphoreType.DMA,
        ],
        compiler_params=pltpu.CompilerParams(vmem_limit_bytes=16 << 20),
        cost_estimate=pl.CostEstimate(flops=rows, bytes_accessed=rows, transcendentals=0),
    )(kept, blocks, total, spread)


def prepare_kernel(tiles, width, kept_ref, coef_ref, flat_ref, blocks_ref, shares_ref, lines, square, partial):
    pairs, slots, flat = flat_ref.shape
    count, share, _ = shares_ref.shape
    length = flat // LANES
    parts = width * 4 // LANES
    spare = LANES - width
    partial[...] = jnp.zeros_like(partial)
    scales = coef_ref[...].astype(jnp.float32)
    lane = lax.broadcasted_iota(jnp.int32, (width // 4, LANES), 1)
    foot = jnp.zeros((spare, LANES), jnp.bfloat16)
    for pair in range(pairs):
        for t in range(length):
            lines[pair, pl.ds(t, slots, stride=length), :] = flat_ref[pair, :, t * LANES:(t + 1) * LANES].astype(jnp.float32)
        for slot in range(slots):
            r = pair * slots + slot
            first, second, third = (lines[pair, pl.ds(slot * length + i, width // 4, stride=parts), :] for i in range(parts))
            quarters = (
                first,
                jnp.where(lane < spare, pltpu.roll(first, spare, 1), pltpu.roll(second, spare, 1)),
                jnp.where(lane < 2 * spare, pltpu.roll(second, 2 * spare, 1), pltpu.roll(third, 2 * spare, 1)),
                pltpu.roll(third, width, 1),
            )
            for j in range(4):
                square[r, pl.ds(j, width // 4, stride=4), :] = jnp.where(lane < width, quarters[j], 0.0)
            block = square[r]
            blocks_ref[r, :width, :] = block.astype(jnp.bfloat16)
            blocks_ref[r, width:, :] = foot
            partial[kept_ref[slot, pair]] += block * scales[:, pair:pair + 1]
    for i in range(count):
        begin = i // tiles * share
        shares_ref[i] = partial[i % tiles, begin:begin + share, :]


def prepare(kept, coef, amplitudes, tiles, groups, width):
    pairs, slots, flat = amplitudes.shape
    rows = pairs * slots
    return pl.pallas_call(
        functools.partial(prepare_kernel, tiles, width),
        out_shape=(
            jax.ShapeDtypeStruct((rows, LANES, LANES), jnp.bfloat16),
            jax.ShapeDtypeStruct((groups * tiles, width // groups, LANES), jnp.float32),
        ),
        in_specs=[SMEM, VMEM, VMEM],
        out_specs=(VMEM, VMEM),
        scratch_shapes=[
            pltpu.VMEM((pairs, slots * flat // LANES, LANES), jnp.float32),
            pltpu.VMEM((rows, width, LANES), jnp.float32),
            pltpu.VMEM((tiles, width, LANES), jnp.float32),
        ],
        compiler_params=pltpu.CompilerParams(vmem_limit_bytes=56 << 20),
        cost_estimate=pl.CostEstimate(flops=rows, bytes_accessed=rows, transcendentals=0),
    )(kept, coef, amplitudes)


def hide_kernel(arrived_ref, integral_ref, out_ref):
    width = integral_ref.shape[-1]
    count, share, _ = out_ref.shape
    running = jnp.sum(arrived_ref[...], axis=0)[:, :width].astype(jnp.bfloat16)
    hidden = jnp.dot(running, integral_ref[0], preferred_element_type=jnp.float32).astype(jnp.bfloat16)
    tail = jnp.zeros((share, LANES - width), jnp.bfloat16)
    for i in range(count):
        out_ref[i, :, :width] = hidden
        out_ref[i, :, width:] = tail


def hide(arrived, integral):
    return pl.pallas_call(
        hide_kernel,
        out_shape=jax.ShapeDtypeStruct(arrived.shape, jnp.bfloat16),
        in_specs=[VMEM, VMEM],
        out_specs=VMEM,
        compiler_params=pltpu.CompilerParams(vmem_limit_bytes=8 << 20),
        cost_estimate=pl.CostEstimate(flops=1000, bytes_accessed=1000, transcendentals=0),
    )(arrived, integral)


def on_device(amplitudes, kept, coef, ladder_factor, cycle_integral_tiles):
    pairs, slots, flat = amplitudes.shape
    width = ladder_factor.shape[-1]
    tiles, groups = lax.axis_size("tile"), lax.axis_size("grp")
    across = 1 << ((tiles.bit_length() - 1) // 2)
    rows = pairs * slots
    me = lax.axis_index("tile")
    core = lax.axis_index("grp") % 2

    def to_tile(array, flip):
        return lax.ppermute(array, "tile", [(i, i ^ flip) for i in range(tiles)])

    def to_core(array):
        return lax.ppermute(array, "grp", [(i, i ^ 1) for i in range(groups)])

    names = kept.T
    blocks, shares = prepare(names, coef.reshape(1, pairs), amplitudes, tiles, groups, width)
    arrived = lax.all_to_all(shares, ALL, split_axis=0, concat_axis=0, tiled=True)
    place = me.reshape(1)
    packed = pack_factors(ladder_factor[0])
    mine = lax.dynamic_index_in_dim(packed, core, 0, keepdims=False)
    half = tiles // 2
    halves = {slot: to_tile(mine, slot) for slot in range(1, half)}

    def stage(near, total):
        parts = []
        for slot in near:
            parts += [halves[slot], to_core(halves[slot])] if slot else [packed[0], packed[1]]
        return ladder(near, names, place, blocks, total, parts, tiles, width, pairs, rows)

    total = stage((0,), None)
    first = total
    far = mine
    for up in range(half, tiles, across):
        halves[up] = to_tile(far, up)
    arrived, _ = lax.optimization_barrier((arrived, first))
    hidden = hide(arrived, cycle_integral_tiles)
    spread = lax.all_to_all(hidden, ALL, split_axis=0, concat_axis=0, tiled=True)
    for up in range(half, tiles, across):
        halves[up], _ = lax.optimization_barrier((halves[up], hidden))
        for side in range(1, across):
            halves[up + side] = to_tile(halves[up], side)
    total = stage(tuple(range(1, half)), total)
    for slot in range(half, tiles):
        if slot % across:
            halves[slot], _ = lax.optimization_barrier((halves[slot], total))
    total = stage(tuple(range(half, tiles, across)), total)
    total = stage(tuple(s for s in range(half, tiles) if s % across), total)
    return close(names, blocks, total, spread, tiles, width, amplitudes.shape)


def solution(mesh):
    in_specs = (
        P(("grp", "tile"), None, None),
        P(("grp", "tile"), None),
        P(("grp", "tile")),
        P("tile", None, None, None),
        P("tile", None, None),
    )
    out_specs = P(("grp", "tile"), None, None)
    return jax.shard_map(
        on_device, mesh=mesh, in_specs=in_specs, out_specs=out_specs, check_vma=False
    )
```

```python
import functools

import jax
import jax.numpy as jnp
from jax import lax
from jax.experimental import pallas as pl
from jax.experimental.pallas import tpu as pltpu
from jax.sharding import PartitionSpec as P

LANES = 128
ALL = ("grp", "tile")


def pack_factors(factors):
    count, width, _ = factors.shape
    quads = factors.reshape(count // 4, 4, width, width)
    spare = LANES - width
    pieces = [quads[:, 3, :, i * spare:(i + 1) * spare] for i in range(3)]
    packed = jnp.concatenate([quads[:, :3], jnp.stack(pieces, axis=1)], axis=-1)
    return packed.reshape(2, count // 8 * 3, width, LANES)


def unpack(refs, stacked, beside, width):
    spare = LANES - width
    lane = lax.broadcasted_iota(jnp.int32, (width, LANES), 1)
    number = 0
    for ref in refs:
        for quad in range(ref.shape[0] // 3):
            parts = [ref[quad * 3 + i] for i in range(3)]
            wide = [part.astype(jnp.float32) for part in parts]
            moved = [pltpu.roll(wide[i], spare * (i + 1), 1) for i in range(3)]
            fourth = jnp.where(lane < spare, moved[0], jnp.where(lane < 2 * spare, moved[1], moved[2]))
            parts.append(fourth.astype(jnp.bfloat16))
            for part in parts:
                stacked[number * width:(number + 1) * width, :] = part
                beside[:, number * LANES:(number + 1) * LANES] = part
                number += 1


def ladder_kernel(near, tiles, width, carried, kept_ref, me_ref, blocks_ref, *rest):
    rest = rest[carried:]
    factor_refs, total_ref = rest[:2 * len(near)], rest[2 * len(near)]
    table, counts, jobs, stacked, beside, grown = rest[2 * len(near) + 1:]
    rows = blocks_ref.shape[0]
    most = table.shape[0] // tiles
    me = me_ref[0]
    slots = kept_ref.shape[0]
    for slot in range(tiles):
        counts[slot] = 0
    for r in range(rows):
        slot = kept_ref[r % slots, r // slots] ^ me
        n = counts[slot]
        table[slot * most + n] = r
        counts[slot] = n + 1

    last = jnp.int32(0)
    for number, slot in enumerate(near):
        count = counts[slot]

        def add(i, at, number=number, slot=slot, count=count):
            jobs[3 * at] = number
            jobs[3 * at + 1] = table[slot * most + 2 * i]
            jobs[3 * at + 2] = table[slot * most + jnp.minimum(2 * i + 1, count - 1)]
            return at + 1

        last = lax.fori_loop(0, (count + 1) // 2, add, last)
    for number in range(len(near)):
        unpack(factor_refs[2 * number:2 * number + 2], stacked.at[number], beside.at[number], width)

    factor_count = stacked.shape[1] // width
    step = 4

    def grow(at, side):
        number = jobs[3 * at]
        pair = jnp.concatenate([blocks_ref[jobs[3 * at + 1]], blocks_ref[jobs[3 * at + 2]]], axis=1)
        for q in range(0, factor_count, step):
            inner = jnp.dot(
                stacked[number, q * width:(q + step) * width], pair, preferred_element_type=jnp.float32
            ).astype(jnp.bfloat16)
            for f in range(step):
                part, lanes = inner[f * width:(f + 1) * width], slice((q + f) * LANES, (q + f + 1) * LANES)
                grown[side, 0:width, lanes] = part[:, :LANES]
                grown[side, width:2 * width, lanes] = part[:, LANES:]

    def reduce(at, side):
        total = lax.dot_general(
            grown[side], beside[jobs[3 * at]], (((1,), (1,)), ((), ())), preferred_element_type=jnp.float32
        )
        total_ref[jobs[3 * at + 1]] = total[:width]
        total_ref[jobs[3 * at + 2]] = total[width:]

    def two(i, _):
        first, second = 2 * i, jnp.minimum(2 * i + 1, last - 1)
        grow(first, 0)
        grow(second, 1)
        reduce(first, 0)
        reduce(second, 1)
        return 0

    lax.fori_loop(0, (last + 1) // 2, two, 0)


SMEM, VMEM = pl.BlockSpec(memory_space=pltpu.SMEM), pl.BlockSpec(memory_space=pltpu.VMEM)
FREE = pl.BlockSpec(memory_space=pl.ANY)


def ladder(near, kept, me, blocks, total, parts, tiles, width, most, cost):
    rows = blocks.shape[0]
    factor_count = parts[0].shape[0] // 3 * 4 * 2
    carried = [] if total is None else [total]
    return pl.pallas_call(
        functools.partial(ladder_kernel, near, tiles, width, len(carried)),
        out_shape=jax.ShapeDtypeStruct((rows, width, width), jnp.float32),
        in_specs=[SMEM, SMEM] + [VMEM] * (1 + len(carried)) + [VMEM] * len(parts),
        out_specs=VMEM,
        input_output_aliases={} if total is None else {3: 0},
        scratch_shapes=[
            pltpu.SMEM((tiles * most,), jnp.int32),
            pltpu.SMEM((tiles,), jnp.int32),
            pltpu.SMEM((3 * (rows + tiles),), jnp.int32),
            pltpu.VMEM((len(near), factor_count * width, LANES), jnp.bfloat16),
            pltpu.VMEM((len(near), width, factor_count * LANES), jnp.bfloat16),
            pltpu.VMEM((2, 2 * width, factor_count * LANES), jnp.bfloat16),
        ],
        compiler_params=pltpu.CompilerParams(vmem_limit_bytes=24 << 20),
        cost_estimate=pl.CostEstimate(flops=cost, bytes_accessed=rows, transcendentals=0),
    )(kept, me, blocks, *carried, *parts)


def close_kernel(tiles, width, kept_ref, blocks_ref, total_ref, spread_ref, out_ref, hidden, square, lines):
    groups = spread_ref.shape[0] // tiles
    pairs, slots, flat = out_ref.shape
    count = flat // LANES
    parts = width * 4 // LANES
    hidden[:, width:, :] = jnp.zeros((tiles, LANES - width, LANES), jnp.bfloat16)
    for tile in range(tiles):
        pieces = [spread_ref[g * tiles + tile].astype(jnp.float32) for g in range(groups)]
        hidden[tile, :width, :] = jnp.concatenate(pieces, axis=0).astype(jnp.bfloat16)
    spare = LANES - width
    lane = lax.broadcasted_iota(jnp.int32, (width // 4, LANES), 1)
    for pair in range(pairs):
        for slot in range(slots):
            r = pair * slots + slot
            term = jnp.dot(blocks_ref[r, :width, :], hidden[kept_ref[slot, pair]], preferred_element_type=jnp.float32)
            square[r, :, :width] = total_ref[r] + term[:, :width]
            quarter = [square[r, pl.ds(j, width // 4, stride=4), :] for j in range(4)]
            second = pltpu.roll(quarter[1], width, 1)
            third = pltpu.roll(quarter[2], 2 * spare, 1)
            fourth = pltpu.roll(quarter[3], spare, 1)
            packed = (
                jnp.where(lane < width, quarter[0], second),
                jnp.where(lane < 2 * spare, second, third),
                jnp.where(lane < spare, third, fourth),
            )
            for i in range(parts):
                lines[pair, pl.ds(slot * count + i, width // 4, stride=parts), :] = packed[i]
        for t in range(count):
            out_ref[pair, :, t * LANES:(t + 1) * LANES] = lines[pair, pl.ds(t, slots, stride=count), :].astype(jnp.bfloat16)


def close(kept, blocks, total, spread, tiles, width, shape):
    rows = blocks.shape[0]
    return pl.pallas_call(
        functools.partial(close_kernel, tiles, width),
        out_shape=jax.ShapeDtypeStruct(shape, jnp.bfloat16),
        in_specs=[SMEM] + [VMEM] * 3,
        out_specs=VMEM,
        scratch_shapes=[
            pltpu.VMEM((tiles, LANES, LANES), jnp.bfloat16),
            pltpu.VMEM((rows, width, LANES), jnp.float32),
            pltpu.VMEM((shape[0], shape[1] * shape[2] // LANES, LANES), jnp.float32),
        ],
        compiler_params=pltpu.CompilerParams(vmem_limit_bytes=16 << 20),
        cost_estimate=pl.CostEstimate(flops=rows, bytes_accessed=rows, transcendentals=0),
    )(kept, blocks, total, spread)


def prepare_kernel(tiles, width, kept_ref, coef_ref, flat_ref, blocks_ref, shares_ref, lines, square, partial):
    pairs, slots, flat = flat_ref.shape
    count, share, _ = shares_ref.shape
    length = flat // LANES
    parts = width * 4 // LANES
    spare = LANES - width
    partial[...] = jnp.zeros_like(partial)
    scales = coef_ref[...].astype(jnp.float32)
    lane = lax.broadcasted_iota(jnp.int32, (width // 4, LANES), 1)
    foot = jnp.zeros((spare, LANES), jnp.bfloat16)
    for pair in range(pairs):
        for t in range(length):
            lines[pair, pl.ds(t, slots, stride=length), :] = flat_ref[pair, :, t * LANES:(t + 1) * LANES].astype(jnp.float32)
        for slot in range(slots):
            r = pair * slots + slot
            first, second, third = (lines[pair, pl.ds(slot * length + i, width // 4, stride=parts), :] for i in range(parts))
            quarters = (
                first,
                jnp.where(lane < spare, pltpu.roll(first, spare, 1), pltpu.roll(second, spare, 1)),
                jnp.where(lane < 2 * spare, pltpu.roll(second, 2 * spare, 1), pltpu.roll(third, 2 * spare, 1)),
                pltpu.roll(third, width, 1),
            )
            for j in range(4):
                square[r, pl.ds(j, width // 4, stride=4), :] = jnp.where(lane < width, quarters[j], 0.0)
            block = square[r]
            blocks_ref[r, :width, :] = block.astype(jnp.bfloat16)
            blocks_ref[r, width:, :] = foot
            partial[kept_ref[slot, pair]] += block * scales[:, pair:pair + 1]
    for i in range(count):
        begin = i // tiles * share
        shares_ref[i] = partial[i % tiles, begin:begin + share, :]


def prepare(kept, coef, amplitudes, tiles, groups, width):
    pairs, slots, flat = amplitudes.shape
    rows = pairs * slots
    return pl.pallas_call(
        functools.partial(prepare_kernel, tiles, width),
        out_shape=(
            jax.ShapeDtypeStruct((rows, LANES, LANES), jnp.bfloat16),
            jax.ShapeDtypeStruct((groups * tiles, width // groups, LANES), jnp.float32),
        ),
        in_specs=[SMEM, VMEM, VMEM],
        out_specs=(VMEM, VMEM),
        scratch_shapes=[
            pltpu.VMEM((pairs, slots * flat // LANES, LANES), jnp.float32),
            pltpu.VMEM((rows, width, LANES), jnp.float32),
            pltpu.VMEM((tiles, width, LANES), jnp.float32),
        ],
        compiler_params=pltpu.CompilerParams(vmem_limit_bytes=56 << 20),
        cost_estimate=pl.CostEstimate(flops=rows, bytes_accessed=rows, transcendentals=0),
    )(kept, coef, amplitudes)


def hide_kernel(arrived_ref, integral_ref, out_ref):
    width = integral_ref.shape[-1]
    count, share, _ = out_ref.shape
    running = jnp.sum(arrived_ref[...], axis=0)[:, :width].astype(jnp.bfloat16)
    hidden = jnp.dot(running, integral_ref[0], preferred_element_type=jnp.float32).astype(jnp.bfloat16)
    tail = jnp.zeros((share, LANES - width), jnp.bfloat16)
    for i in range(count):
        out_ref[i, :, :width] = hidden
        out_ref[i, :, width:] = tail


def hide(arrived, integral):
    return pl.pallas_call(
        hide_kernel,
        out_shape=jax.ShapeDtypeStruct(arrived.shape, jnp.bfloat16),
        in_specs=[VMEM, VMEM],
        out_specs=VMEM,
        compiler_params=pltpu.CompilerParams(vmem_limit_bytes=8 << 20),
        cost_estimate=pl.CostEstimate(flops=1000, bytes_accessed=1000, transcendentals=0),
    )(arrived, integral)


def on_device(amplitudes, kept, coef, ladder_factor, cycle_integral_tiles):
    pairs, slots, flat = amplitudes.shape
    width = ladder_factor.shape[-1]
    tiles, groups = lax.axis_size("tile"), lax.axis_size("grp")
    across = 1 << ((tiles.bit_length() - 1) // 2)
    rows = pairs * slots
    me = lax.axis_index("tile")
    core = lax.axis_index("grp") % 2

    def to_tile(array, flip):
        return lax.ppermute(array, "tile", [(i, i ^ flip) for i in range(tiles)])

    def to_core(array):
        return lax.ppermute(array, "grp", [(i, i ^ 1) for i in range(groups)])

    names = kept.T
    blocks, shares = prepare(names, coef.reshape(1, pairs), amplitudes, tiles, groups, width)
    arrived = lax.all_to_all(shares, ALL, split_axis=0, concat_axis=0, tiled=True)
    place = me.reshape(1)
    packed = pack_factors(ladder_factor[0])
    mine = lax.dynamic_index_in_dim(packed, core, 0, keepdims=False)
    half = tiles // 2
    halves = {slot: to_tile(mine, slot) for slot in range(1, half)}

    def stage(near, total):
        parts = []
        for slot in near:
            parts += [halves[slot], to_core(halves[slot])] if slot else [packed[0], packed[1]]
        return ladder(near, names, place, blocks, total, parts, tiles, width, pairs, rows)

    total = stage((0,), None)
    first = total
    far = mine
    for up in range(half, tiles, across):
        halves[up] = to_tile(far, up)
    arrived, _ = lax.optimization_barrier((arrived, first))
    hidden = hide(arrived, cycle_integral_tiles)
    spread = lax.all_to_all(hidden, ALL, split_axis=0, concat_axis=0, tiled=True)
    for up in range(half, tiles, across):
        halves[up], _ = lax.optimization_barrier((halves[up], hidden))
        for side in range(1, across):
            halves[up + side] = to_tile(halves[up], side)
    total = stage(tuple(range(1, half)), total)
    for slot in range(half, tiles):
        if slot % across:
            halves[slot], _ = lax.optimization_barrier((halves[slot], total))
    total = stage(tuple(range(half, tiles, across)), total)
    total = stage(tuple(s for s in range(half, tiles) if s % across), total)
    return close(names, blocks, total, spread, tiles, width, amplitudes.shape)


def solution(mesh):
    in_specs = (
        P(("grp", "tile"), None, None),
        P(("grp", "tile"), None),
        P(("grp", "tile")),
        P("tile", None, None, None),
        P("tile", None, None),
    )
    out_specs = P(("grp", "tile"), None, None)
    return jax.shard_map(
        on_device, mesh=mesh, in_specs=in_specs, out_specs=out_specs, check_vma=False
    )
```

```python
import functools

import jax
import jax.numpy as jnp
from jax import lax
from jax.experimental import pallas as pl
from jax.experimental.pallas import tpu as pltpu
from jax.sharding import PartitionSpec as P

LANES = 128
ALL = ("grp", "tile")


def pack_factors(factors):
    count, width, _ = factors.shape
    quads = factors.reshape(count // 4, 4, width, width)
    spare = LANES - width
    pieces = [quads[:, 3, :, i * spare:(i + 1) * spare] for i in range(3)]
    packed = jnp.concatenate([quads[:, :3], jnp.stack(pieces, axis=1)], axis=-1)
    return packed.reshape(2, count // 8 * 3, width, LANES)


def unpack(refs, stacked, beside, width):
    spare = LANES - width
    lane = lax.broadcasted_iota(jnp.int32, (width, LANES), 1)
    number = 0
    for ref in refs:
        for quad in range(ref.shape[0] // 3):
            parts = [ref[quad * 3 + i] for i in range(3)]
            wide = [part.astype(jnp.float32) for part in parts]
            moved = [pltpu.roll(wide[i], spare * (i + 1), 1) for i in range(3)]
            fourth = jnp.where(lane < spare, moved[0], jnp.where(lane < 2 * spare, moved[1], moved[2]))
            parts.append(fourth.astype(jnp.bfloat16))
            for part in parts:
                stacked[number * width:(number + 1) * width, :] = part
                beside[:, number * LANES:(number + 1) * LANES] = part
                number += 1


def ladder_kernel(near, tiles, width, carried, kept_ref, me_ref, blocks_ref, *rest):
    rest = rest[carried:]
    factor_refs, total_ref = rest[:2 * len(near)], rest[2 * len(near)]
    table, counts, jobs, stacked, beside, grown = rest[2 * len(near) + 1:]
    rows = blocks_ref.shape[0]
    most = table.shape[0] // tiles
    me = me_ref[0]
    slots = kept_ref.shape[0]
    for slot in range(tiles):
        counts[slot] = 0
    for r in range(rows):
        slot = kept_ref[r % slots, r // slots] ^ me
        n = counts[slot]
        table[slot * most + n] = r
        counts[slot] = n + 1

    last = jnp.int32(0)
    for number, slot in enumerate(near):
        count = counts[slot]

        def add(i, at, number=number, slot=slot, count=count):
            jobs[3 * at] = number
            jobs[3 * at + 1] = table[slot * most + 2 * i]
            jobs[3 * at + 2] = table[slot * most + jnp.minimum(2 * i + 1, count - 1)]
            return at + 1

        last = lax.fori_loop(0, (count + 1) // 2, add, last)
    for number in range(len(near)):
        unpack(factor_refs[2 * number:2 * number + 2], stacked.at[number], beside.at[number], width)

    factor_count = stacked.shape[1] // width
    step = 4

    def grow(at, side):
        number = jobs[3 * at]
        pair = jnp.concatenate([blocks_ref[jobs[3 * at + 1]], blocks_ref[jobs[3 * at + 2]]], axis=1)
        for q in range(0, factor_count, step):
            inner = jnp.dot(
                stacked[number, q * width:(q + step) * width], pair, preferred_element_type=jnp.float32
            ).astype(jnp.bfloat16)
            for f in range(step):
                part, lanes = inner[f * width:(f + 1) * width], slice((q + f) * LANES, (q + f + 1) * LANES)
                grown[side, 0:width, lanes] = part[:, :LANES]
                grown[side, width:2 * width, lanes] = part[:, LANES:]

    def reduce(at, side):
        total = lax.dot_general(
            grown[side], beside[jobs[3 * at]], (((1,), (1,)), ((), ())), preferred_element_type=jnp.float32
        )
        total_ref[jobs[3 * at + 1]] = total[:width]
        total_ref[jobs[3 * at + 2]] = total[width:]

    def two(i, _):
        first, second = 2 * i, jnp.minimum(2 * i + 1, last - 1)
        grow(first, 0)
        grow(second, 1)
        reduce(first, 0)
        reduce(second, 1)
        return 0

    lax.fori_loop(0, (last + 1) // 2, two, 0)


SMEM, VMEM = pl.BlockSpec(memory_space=pltpu.SMEM), pl.BlockSpec(memory_space=pltpu.VMEM)
FREE = pl.BlockSpec(memory_space=pl.ANY)


def ladder(near, kept, me, blocks, total, parts, tiles, width, most, cost):
    rows = blocks.shape[0]
    factor_count = parts[0].shape[0] // 3 * 4 * 2
    carried = [] if total is None else [total]
    return pl.pallas_call(
        functools.partial(ladder_kernel, near, tiles, width, len(carried)),
        out_shape=jax.ShapeDtypeStruct((rows, width, width), jnp.float32),
        in_specs=[SMEM, SMEM] + [VMEM] * (1 + len(carried)) + [VMEM] * len(parts),
        out_specs=VMEM,
        input_output_aliases={} if total is None else {3: 0},
        scratch_shapes=[
            pltpu.SMEM((tiles * most,), jnp.int32),
            pltpu.SMEM((tiles,), jnp.int32),
            pltpu.SMEM((3 * (rows + tiles),), jnp.int32),
            pltpu.VMEM((len(near), factor_count * width, LANES), jnp.bfloat16),
            pltpu.VMEM((len(near), width, factor_count * LANES), jnp.bfloat16),
            pltpu.VMEM((2, 2 * width, factor_count * LANES), jnp.bfloat16),
        ],
        compiler_params=pltpu.CompilerParams(vmem_limit_bytes=24 << 20),
        cost_estimate=pl.CostEstimate(flops=cost, bytes_accessed=rows, transcendentals=0),
    )(kept, me, blocks, *carried, *parts)


def close_kernel(tiles, width, kept_ref, blocks_ref, total_ref, spread_ref, out_ref, hidden, square, lines):
    groups = spread_ref.shape[0] // tiles
    pairs, slots, flat = out_ref.shape
    count = flat // LANES
    parts = width * 4 // LANES
    hidden[:, width:, :] = jnp.zeros((tiles, LANES - width, LANES), jnp.bfloat16)
    for tile in range(tiles):
        pieces = [spread_ref[g * tiles + tile].astype(jnp.float32) for g in range(groups)]
        hidden[tile, :width, :] = jnp.concatenate(pieces, axis=0).astype(jnp.bfloat16)
    spare = LANES - width
    lane = lax.broadcasted_iota(jnp.int32, (width // 4, LANES), 1)
    for pair in range(pairs):
        for slot in range(slots):
            r = pair * slots + slot
            term = jnp.dot(blocks_ref[r, :width, :], hidden[kept_ref[slot, pair]], preferred_element_type=jnp.float32)
            square[r, :, :width] = total_ref[r] + term[:, :width]
            quarter = [square[r, pl.ds(j, width // 4, stride=4), :] for j in range(4)]
            second = pltpu.roll(quarter[1], width, 1)
            third = pltpu.roll(quarter[2], 2 * spare, 1)
            fourth = pltpu.roll(quarter[3], spare, 1)
            packed = (
                jnp.where(lane < width, quarter[0], second),
                jnp.where(lane < 2 * spare, second, third),
                jnp.where(lane < spare, third, fourth),
            )
            for i in range(parts):
                lines[pair // 2, pl.ds((pair % 2 * slots + slot) * count + i, width // 4, stride=parts), :] = packed[i]
        if pair % 2:
            for t in range(count):
                both = lines[pair // 2, pl.ds(t, 2 * slots, stride=count), :].astype(jnp.bfloat16)
                out_ref[pair - 1, :, t * LANES:(t + 1) * LANES] = both[:slots]
                out_ref[pair, :, t * LANES:(t + 1) * LANES] = both[slots:]


def close(kept, blocks, total, spread, tiles, width, shape):
    rows = blocks.shape[0]
    return pl.pallas_call(
        functools.partial(close_kernel, tiles, width),
        out_shape=jax.ShapeDtypeStruct(shape, jnp.bfloat16),
        in_specs=[SMEM] + [VMEM] * 3,
        out_specs=VMEM,
        scratch_shapes=[
            pltpu.VMEM((tiles, LANES, LANES), jnp.bfloat16),
            pltpu.VMEM((rows, width, LANES), jnp.float32),
            pltpu.VMEM((shape[0] // 2, 2 * shape[1] * shape[2] // LANES, LANES), jnp.float32),
        ],
        compiler_params=pltpu.CompilerParams(vmem_limit_bytes=16 << 20),
        cost_estimate=pl.CostEstimate(flops=rows, bytes_accessed=rows, transcendentals=0),
    )(kept, blocks, total, spread)


def prepare_kernel(tiles, width, kept_ref, coef_ref, flat_ref, blocks_ref, shares_ref, lines, square, partial):
    pairs, slots, flat = flat_ref.shape
    count, share, _ = shares_ref.shape
    length = flat // LANES
    parts = width * 4 // LANES
    spare = LANES - width
    partial[...] = jnp.zeros_like(partial)
    scales = coef_ref[...].astype(jnp.float32)
    lane = lax.broadcasted_iota(jnp.int32, (width // 4, LANES), 1)
    foot = jnp.zeros((spare, LANES), jnp.bfloat16)
    for pair in range(pairs):
        for t in range(length if pair % 2 == 0 else 0):
            lanes = slice(t * LANES, (t + 1) * LANES)
            both = [flat_ref[pair + i, :, lanes].astype(jnp.float32) for i in range(2)]
            lines[pair // 2, pl.ds(t, 2 * slots, stride=length), :] = jnp.concatenate(both, axis=0)
        for slot in range(slots):
            r = pair * slots + slot
            first, second, third = (lines[pair // 2, pl.ds((pair % 2 * slots + slot) * length + i, width // 4, stride=parts), :] for i in range(parts))
            quarters = (
                first,
                jnp.where(lane < spare, pltpu.roll(first, spare, 1), pltpu.roll(second, spare, 1)),
                jnp.where(lane < 2 * spare, pltpu.roll(second, 2 * spare, 1), pltpu.roll(third, 2 * spare, 1)),
                pltpu.roll(third, width, 1),
            )
            for j in range(4):
                square[r, pl.ds(j, width // 4, stride=4), :] = jnp.where(lane < width, quarters[j], 0.0)
            block = square[r]
            blocks_ref[r, :width, :] = block.astype(jnp.bfloat16)
            blocks_ref[r, width:, :] = foot
            partial[kept_ref[slot, pair]] += block * scales[:, pair:pair + 1]
    for i in range(count):
        begin = i // tiles * share
        shares_ref[i] = partial[i % tiles, begin:begin + share, :]


def prepare(kept, coef, amplitudes, tiles, groups, width):
    pairs, slots, flat = amplitudes.shape
    rows = pairs * slots
    return pl.pallas_call(
        functools.partial(prepare_kernel, tiles, width),
        out_shape=(
            jax.ShapeDtypeStruct((rows, LANES, LANES), jnp.bfloat16),
            jax.ShapeDtypeStruct((groups * tiles, width // groups, LANES), jnp.float32),
        ),
        in_specs=[SMEM, VMEM, VMEM],
        out_specs=(VMEM, VMEM),
        scratch_shapes=[
            pltpu.VMEM((pairs // 2, 2 * slots * flat // LANES, LANES), jnp.float32),
            pltpu.VMEM((rows, width, LANES), jnp.float32),
            pltpu.VMEM((tiles, width, LANES), jnp.float32),
        ],
        compiler_params=pltpu.CompilerParams(vmem_limit_bytes=56 << 20),
        cost_estimate=pl.CostEstimate(flops=rows, bytes_accessed=rows, transcendentals=0),
    )(kept, coef, amplitudes)


def hide_kernel(arrived_ref, integral_ref, out_ref):
    width = integral_ref.shape[-1]
    count, share, _ = out_ref.shape
    running = jnp.sum(arrived_ref[...], axis=0)[:, :width].astype(jnp.bfloat16)
    hidden = jnp.dot(running, integral_ref[0], preferred_element_type=jnp.float32).astype(jnp.bfloat16)
    tail = jnp.zeros((share, LANES - width), jnp.bfloat16)
    for i in range(count):
        out_ref[i, :, :width] = hidden
        out_ref[i, :, width:] = tail


def hide(arrived, integral):
    return pl.pallas_call(
        hide_kernel,
        out_shape=jax.ShapeDtypeStruct(arrived.shape, jnp.bfloat16),
        in_specs=[VMEM, VMEM],
        out_specs=VMEM,
        compiler_params=pltpu.CompilerParams(vmem_limit_bytes=8 << 20),
        cost_estimate=pl.CostEstimate(flops=1000, bytes_accessed=1000, transcendentals=0),
    )(arrived, integral)


def on_device(amplitudes, kept, coef, ladder_factor, cycle_integral_tiles):
    pairs, slots, flat = amplitudes.shape
    width = ladder_factor.shape[-1]
    tiles, groups = lax.axis_size("tile"), lax.axis_size("grp")
    across = 1 << ((tiles.bit_length() - 1) // 2)
    rows = pairs * slots
    me = lax.axis_index("tile")
    core = lax.axis_index("grp") % 2

    def to_tile(array, flip):
        return lax.ppermute(array, "tile", [(i, i ^ flip) for i in range(tiles)])

    def to_core(array):
        return lax.ppermute(array, "grp", [(i, i ^ 1) for i in range(groups)])

    names = kept.T
    blocks, shares = prepare(names, coef.reshape(1, pairs), amplitudes, tiles, groups, width)
    arrived = lax.all_to_all(shares, ALL, split_axis=0, concat_axis=0, tiled=True)
    place = me.reshape(1)
    packed = pack_factors(ladder_factor[0])
    mine = lax.dynamic_index_in_dim(packed, core, 0, keepdims=False)
    half = tiles // 2
    halves = {slot: to_tile(mine, slot) for slot in range(1, half)}

    def stage(near, total):
        parts = []
        for slot in near:
            parts += [halves[slot], to_core(halves[slot])] if slot else [packed[0], packed[1]]
        return ladder(near, names, place, blocks, total, parts, tiles, width, pairs, rows)

    total = stage((0,), None)
    first = total
    far = mine
    for up in range(half, tiles, across):
        halves[up] = to_tile(far, up)
    arrived, _ = lax.optimization_barrier((arrived, first))
    hidden = hide(arrived, cycle_integral_tiles)
    spread = lax.all_to_all(hidden, ALL, split_axis=0, concat_axis=0, tiled=True)
    for up in range(half, tiles, across):
        halves[up], _ = lax.optimization_barrier((halves[up], hidden))
        for side in range(1, across):
            halves[up + side] = to_tile(halves[up], side)
    total = stage(tuple(range(1, half)), total)
    for slot in range(half, tiles):
        if slot % across:
            halves[slot], _ = lax.optimization_barrier((halves[slot], total))
    total = stage(tuple(range(half, tiles, across)), total)
    total = stage(tuple(s for s in range(half, tiles) if s % across), total)
    return close(names, blocks, total, spread, tiles, width, amplitudes.shape)


def solution(mesh):
    in_specs = (
        P(("grp", "tile"), None, None),
        P(("grp", "tile"), None),
        P(("grp", "tile")),
        P("tile", None, None, None),
        P("tile", None, None),
    )
    out_specs = P(("grp", "tile"), None, None)
    return jax.shard_map(
        on_device, mesh=mesh, in_specs=in_specs, out_specs=out_specs, check_vma=False
    )
```

```python
import functools

import jax
import jax.numpy as jnp
from jax import lax
from jax.experimental import pallas as pl
from jax.experimental.pallas import tpu as pltpu
from jax.sharding import PartitionSpec as P

LANES = 128
ALL = ("grp", "tile")


def pack_factors(factors):
    count, width, _ = factors.shape
    quads = factors.reshape(count // 4, 4, width, width)
    spare = LANES - width
    pieces = [quads[:, 3, :, i * spare:(i + 1) * spare] for i in range(3)]
    packed = jnp.concatenate([quads[:, :3], jnp.stack(pieces, axis=1)], axis=-1)
    return packed.reshape(2, count // 8 * 3, width, LANES)


def unpack(refs, stacked, beside, width):
    spare = LANES - width
    lane = lax.broadcasted_iota(jnp.int32, (width, LANES), 1)
    number = 0
    for ref in refs:
        for quad in range(ref.shape[0] // 3):
            parts = [ref[quad * 3 + i] for i in range(3)]
            wide = [part.astype(jnp.float32) for part in parts]
            moved = [pltpu.roll(wide[i], spare * (i + 1), 1) for i in range(3)]
            fourth = jnp.where(lane < spare, moved[0], jnp.where(lane < 2 * spare, moved[1], moved[2]))
            parts.append(fourth.astype(jnp.bfloat16))
            for part in parts:
                stacked[number * width:(number + 1) * width, :] = part
                beside[:, number * LANES:(number + 1) * LANES] = part
                number += 1


def ladder_kernel(near, tiles, width, carried, kept_ref, me_ref, blocks_ref, *rest):
    rest = rest[carried:]
    factor_refs, total_ref = rest[:2 * len(near)], rest[2 * len(near)]
    table, counts, jobs, stacked, beside, grown = rest[2 * len(near) + 1:]
    rows = blocks_ref.shape[0]
    most = table.shape[0] // tiles
    me = me_ref[0]
    slots = kept_ref.shape[0]
    for slot in range(tiles):
        counts[slot] = 0
    for r in range(rows):
        slot = kept_ref[r % slots, r // slots] ^ me
        n = counts[slot]
        table[slot * most + n] = r
        counts[slot] = n + 1

    last = jnp.int32(0)
    for number, slot in enumerate(near):
        count = counts[slot]

        def add(i, at, number=number, slot=slot, count=count):
            jobs[3 * at] = number
            jobs[3 * at + 1] = table[slot * most + 2 * i]
            jobs[3 * at + 2] = table[slot * most + jnp.minimum(2 * i + 1, count - 1)]
            return at + 1

        last = lax.fori_loop(0, (count + 1) // 2, add, last)
    for number in range(len(near)):
        unpack(factor_refs[2 * number:2 * number + 2], stacked.at[number], beside.at[number], width)

    factor_count = stacked.shape[1] // width
    step = 4

    def grow(at, side):
        number = jobs[3 * at]
        pair = jnp.concatenate([blocks_ref[jobs[3 * at + 1]], blocks_ref[jobs[3 * at + 2]]], axis=1)
        for q in range(0, factor_count, step):
            inner = jnp.dot(
                stacked[number, q * width:(q + step) * width], pair, preferred_element_type=jnp.float32
            ).astype(jnp.bfloat16)
            for f in range(step):
                part, lanes = inner[f * width:(f + 1) * width], slice((q + f) * LANES, (q + f + 1) * LANES)
                grown[side, 0:width, lanes] = part[:, :LANES]
                grown[side, width:2 * width, lanes] = part[:, LANES:]

    def reduce(at, side):
        total = lax.dot_general(
            grown[side], beside[jobs[3 * at]], (((1,), (1,)), ((), ())), preferred_element_type=jnp.float32
        )
        total_ref[jobs[3 * at + 1]] = total[:width]
        total_ref[jobs[3 * at + 2]] = total[width:]

    def two(i, _):
        first, second = 2 * i, jnp.minimum(2 * i + 1, last - 1)
        grow(first, 0)
        grow(second, 1)
        reduce(first, 0)
        reduce(second, 1)
        return 0

    lax.fori_loop(0, (last + 1) // 2, two, 0)


SMEM, VMEM = pl.BlockSpec(memory_space=pltpu.SMEM), pl.BlockSpec(memory_space=pltpu.VMEM)
FREE = pl.BlockSpec(memory_space=pl.ANY)


def ladder(near, kept, me, blocks, total, parts, tiles, width, most, cost):
    rows = blocks.shape[0]
    factor_count = parts[0].shape[0] // 3 * 4 * 2
    carried = [] if total is None else [total]
    return pl.pallas_call(
        functools.partial(ladder_kernel, near, tiles, width, len(carried)),
        out_shape=jax.ShapeDtypeStruct((rows, width, width), jnp.float32),
        in_specs=[SMEM, SMEM] + [VMEM] * (1 + len(carried)) + [VMEM] * len(parts),
        out_specs=VMEM,
        input_output_aliases={} if total is None else {3: 0},
        scratch_shapes=[
            pltpu.SMEM((tiles * most,), jnp.int32),
            pltpu.SMEM((tiles,), jnp.int32),
            pltpu.SMEM((3 * (rows + tiles),), jnp.int32),
            pltpu.VMEM((len(near), factor_count * width, LANES), jnp.bfloat16),
            pltpu.VMEM((len(near), width, factor_count * LANES), jnp.bfloat16),
            pltpu.VMEM((2, 2 * width, factor_count * LANES), jnp.bfloat16),
        ],
        compiler_params=pltpu.CompilerParams(vmem_limit_bytes=24 << 20),
        cost_estimate=pl.CostEstimate(flops=cost, bytes_accessed=rows, transcendentals=0),
    )(kept, me, blocks, *carried, *parts)


def close_kernel(tiles, width, kept_ref, blocks_ref, total_ref, spread_ref, out_ref, hidden, square, lines):
    groups = spread_ref.shape[0] // tiles
    pairs, slots, flat = out_ref.shape
    count = flat // LANES
    parts = width * 4 // LANES
    hidden[:, width:, :] = jnp.zeros((tiles, LANES - width, LANES), jnp.bfloat16)
    for tile in range(tiles):
        pieces = [spread_ref[g * tiles + tile].astype(jnp.float32) for g in range(groups)]
        hidden[tile, :width, :] = jnp.concatenate(pieces, axis=0).astype(jnp.bfloat16)
    spare = LANES - width
    lane = lax.broadcasted_iota(jnp.int32, (width // 4, LANES), 1)
    for pair in range(pairs):
        for slot in range(slots):
            r = pair * slots + slot
            term = jnp.dot(blocks_ref[r, :width, :], hidden[kept_ref[slot, pair]], preferred_element_type=jnp.float32)
            square[r, :, :width] = total_ref[r] + term[:, :width]
            quarter = [square[r, pl.ds(j, width // 4, stride=4), :] for j in range(4)]
            second = pltpu.roll(quarter[1], width, 1)
            third = pltpu.roll(quarter[2], 2 * spare, 1)
            fourth = pltpu.roll(quarter[3], spare, 1)
            packed = (
                jnp.where(lane < width, quarter[0], second),
                jnp.where(lane < 2 * spare, second, third),
                jnp.where(lane < spare, third, fourth),
            )
            for i in range(parts):
                lines[pair // 2, pl.ds((pair % 2 * slots + slot) * count + i, width // 4, stride=parts), :] = packed[i]
        if pair % 2:
            for t in range(count):
                both = lines[pair // 2, pl.ds(t, 2 * slots, stride=count), :].astype(jnp.bfloat16)
                out_ref[pair - 1, :, t * LANES:(t + 1) * LANES] = both[:slots]
                out_ref[pair, :, t * LANES:(t + 1) * LANES] = both[slots:]


def close(kept, blocks, total, spread, tiles, width, shape):
    rows = blocks.shape[0]
    return pl.pallas_call(
        functools.partial(close_kernel, tiles, width),
        out_shape=jax.ShapeDtypeStruct(shape, jnp.bfloat16),
        in_specs=[SMEM] + [VMEM] * 3,
        out_specs=VMEM,
        scratch_shapes=[
            pltpu.VMEM((tiles, LANES, LANES), jnp.bfloat16),
            pltpu.VMEM((rows, width, LANES), jnp.float32),
            pltpu.VMEM((shape[0] // 2, 2 * shape[1] * shape[2] // LANES, LANES), jnp.float32),
        ],
        compiler_params=pltpu.CompilerParams(vmem_limit_bytes=16 << 20),
        cost_estimate=pl.CostEstimate(flops=rows, bytes_accessed=rows, transcendentals=0),
    )(kept, blocks, total, spread)


def prepare_kernel(tiles, width, kept_ref, coef_ref, flat_ref, blocks_ref, shares_ref, lines, square, partial):
    pairs, slots, flat = flat_ref.shape
    count, share, _ = shares_ref.shape
    length = flat // LANES
    parts = width * 4 // LANES
    spare = LANES - width
    partial[...] = jnp.zeros_like(partial)
    scales = coef_ref[...].astype(jnp.float32)
    lane = lax.broadcasted_iota(jnp.int32, (width // 4, LANES), 1)
    foot = jnp.zeros((spare, LANES), jnp.bfloat16)
    for pair in range(pairs):
        for t in range(length if pair % 2 == 0 else 0):
            lanes = slice(t * LANES, (t + 1) * LANES)
            both = [flat_ref[pair + i, :, lanes].astype(jnp.float32) for i in range(2)]
            lines[pair // 2, pl.ds(t, 2 * slots, stride=length), :] = jnp.concatenate(both, axis=0)
        for slot in range(slots):
            r = pair * slots + slot
            first, second, third = (lines[pair // 2, pl.ds((pair % 2 * slots + slot) * length + i, width // 4, stride=parts), :] for i in range(parts))
            quarters = (
                first,
                jnp.where(lane < spare, pltpu.roll(first, spare, 1), pltpu.roll(second, spare, 1)),
                jnp.where(lane < 2 * spare, pltpu.roll(second, 2 * spare, 1), pltpu.roll(third, 2 * spare, 1)),
                pltpu.roll(third, width, 1),
            )
            for j in range(4):
                square[r, pl.ds(j, width // 4, stride=4), :] = jnp.where(lane < width, quarters[j], 0.0)
            block = square[r]
            blocks_ref[r, :width, :] = block.astype(jnp.bfloat16)
            blocks_ref[r, width:, :] = foot
            partial[kept_ref[slot, pair]] += block * scales[:, pair:pair + 1]
    for i in range(count):
        begin = i // tiles * share
        shares_ref[i] = partial[i % tiles, begin:begin + share, :]


def prepare(kept, coef, amplitudes, tiles, groups, width):
    pairs, slots, flat = amplitudes.shape
    rows = pairs * slots
    return pl.pallas_call(
        functools.partial(prepare_kernel, tiles, width),
        out_shape=(
            jax.ShapeDtypeStruct((rows, LANES, LANES), jnp.bfloat16),
            jax.ShapeDtypeStruct((groups * tiles, width // groups, LANES), jnp.float32),
        ),
        in_specs=[SMEM, VMEM, VMEM],
        out_specs=(VMEM, VMEM),
        scratch_shapes=[
            pltpu.VMEM((pairs // 2, 2 * slots * flat // LANES, LANES), jnp.float32),
            pltpu.VMEM((rows, width, LANES), jnp.float32),
            pltpu.VMEM((tiles, width, LANES), jnp.float32),
        ],
        compiler_params=pltpu.CompilerParams(vmem_limit_bytes=56 << 20),
        cost_estimate=pl.CostEstimate(flops=rows, bytes_accessed=rows, transcendentals=0),
    )(kept, coef, amplitudes)


def hide_kernel(arrived_ref, integral_ref, out_ref):
    width = integral_ref.shape[-1]
    count, share, _ = out_ref.shape
    running = jnp.sum(arrived_ref[...], axis=0)[:, :width].astype(jnp.bfloat16)
    hidden = jnp.dot(running, integral_ref[0], preferred_element_type=jnp.float32).astype(jnp.bfloat16)
    tail = jnp.zeros((share, LANES - width), jnp.bfloat16)
    for i in range(count):
        out_ref[i, :, :width] = hidden
        out_ref[i, :, width:] = tail


def hide(arrived, integral):
    return pl.pallas_call(
        hide_kernel,
        out_shape=jax.ShapeDtypeStruct(arrived.shape, jnp.bfloat16),
        in_specs=[VMEM, VMEM],
        out_specs=VMEM,
        compiler_params=pltpu.CompilerParams(vmem_limit_bytes=8 << 20),
        cost_estimate=pl.CostEstimate(flops=1000, bytes_accessed=1000, transcendentals=0),
    )(arrived, integral)


def on_device(amplitudes, kept, coef, ladder_factor, cycle_integral_tiles):
    pairs, slots, flat = amplitudes.shape
    width = ladder_factor.shape[-1]
    tiles, groups = lax.axis_size("tile"), lax.axis_size("grp")
    across = 1 << ((tiles.bit_length() - 1) // 2)
    rows = pairs * slots
    me = lax.axis_index("tile")
    core = lax.axis_index("grp") % 2

    def to_tile(array, flip):
        return lax.ppermute(array, "tile", [(i, i ^ flip) for i in range(tiles)])

    def to_core(array):
        return lax.ppermute(array, "grp", [(i, i ^ 1) for i in range(groups)])

    names = kept.T
    blocks, shares = prepare(names, coef.reshape(1, pairs), amplitudes, tiles, groups, width)
    arrived = lax.all_to_all(shares, ALL, split_axis=0, concat_axis=0, tiled=True)
    place = me.reshape(1)
    packed = pack_factors(ladder_factor[0])
    mine = lax.dynamic_index_in_dim(packed, core, 0, keepdims=False)
    half = tiles // 2
    halves = {slot: to_tile(mine, slot) for slot in range(1, half)}

    def stage(near, total):
        parts = []
        for slot in near:
            parts += [halves[slot], to_core(halves[slot])] if slot else [packed[0], packed[1]]
        return ladder(near, names, place, blocks, total, parts, tiles, width, pairs, rows)

    total = stage((0,), None)
    first = total
    far, _ = lax.optimization_barrier((mine, shares))
    for up in range(half, tiles, across):
        halves[up] = to_tile(far, up)
    arrived, _ = lax.optimization_barrier((arrived, first))
    hidden = hide(arrived, cycle_integral_tiles)
    spread = lax.all_to_all(hidden, ALL, split_axis=0, concat_axis=0, tiled=True)
    for up in range(half, tiles, across):
        halves[up], _ = lax.optimization_barrier((halves[up], hidden))
        for side in range(1, across):
            halves[up + side] = to_tile(halves[up], side)
    total = stage(tuple(range(1, half)), total)
    for slot in range(half, tiles):
        if slot % across:
            halves[slot], _ = lax.optimization_barrier((halves[slot], total))
    total = stage(tuple(range(half, tiles, across)), total)
    total = stage(tuple(s for s in range(half, tiles) if s % across), total)
    return close(names, blocks, total, spread, tiles, width, amplitudes.shape)


def solution(mesh):
    in_specs = (
        P(("grp", "tile"), None, None),
        P(("grp", "tile"), None),
        P(("grp", "tile")),
        P("tile", None, None, None),
        P("tile", None, None),
    )
    out_specs = P(("grp", "tile"), None, None)
    return jax.shard_map(
        on_device, mesh=mesh, in_specs=in_specs, out_specs=out_specs, check_vma=False
    )
```
